128 devices in a mesh: grp: 4 (over z_lo, core), kp: 32 (over x, z_hi, y).
Axes of the slice: x: 4, y: 4, z: 4 (z_hi: 2, z_lo: 2; z = z_hi * 2 + z_lo), core: 2. Of those that a mesh axis runs over, the one named last changes fastest.
Arguments:
- g_real: bfloat16 [2, 1024, 6144], P(None, 'kp'), may hold values from -0.1875 to 0.1875
- lattice: int32 [3, 1024], replicated, may hold values from -20 to 20
- u_rot: float32 [2, 16, 16, 16384], P(None, None, None, ('grp', 'kp')), may hold values from -1.5 to 1.5
- energy: float32 [16, 16384], P(None, ('grp', 'kp')), may hold values from -2 to 2
- band_mask: int32 [16, 16384], P(None, ('grp', 'kp')), may hold values 0 or 1
- freq: float32 [2, 12], replicated, may hold values from 0.01 to 0.1
- froh: float32 [2, 2, 12], replicated, may hold values from -6 to 6
- kq_index: int32 [2, 128], replicated, may hold values from 0 to 127, each once within a row
- irr_id: int32 [16384], P(('grp', 'kp')), may hold values from 0 to 511
Outputs:
- sigma_k: float32 [2, 16, 16384], P(None, None, ('grp', 'kp'))
- sigma_irr: float32 [2, 16, 2048], P(None, None, ('grp', 'kp'))
The draws below stay inside these ranges and needn't reach their ends.
Inputs may be any that keep to these rules, and one draw needn't show every extreme that they name: `kq_index`: each row is a permutation of the positions 0 to 127. `irr_id`: irreducible points are numbered within a block of 4096 k points.
All inputs are finite; a program needn't handle non-finite values. No bound on the sum of `band_mask` on one device may be relied on, other than what follows from the above.
Results may differ from the reference program's by a relative error of at most 0.0027.
Values may be sent and summed in bfloat16 or wider, within the bound.
A program may use at most 192 MiB of HBM per device.

```python
import math
import jax
import jax.numpy as jnp
import numpy as np
from jax import lax

NW = 16
MODES = 12
NR = 1024
QSTEPS = 2
NKM = 40
KDEV = 128
FV = 3072
KGRP = 4096
KPTS = 16384
IRR_GRP = 512
IRR = 2048
N_GRP = 4
N_KP = 32


def with_ends(drawn, own_key, smallest, largest):
    longest = drawn.shape.index(max(drawn.shape))
    spots = []
    for shift in (0, 1):
        where = [jax.random.randint(jax.random.fold_in(own_key, axis), (), 0, length) for axis, length in enumerate(drawn.shape)]
        where[longest] = (where[longest] + shift) % drawn.shape[longest]
        spots.append(tuple(where))
    return drawn.at[spots[0]].set(smallest).at[spots[1]].set(largest)


def block_levels(rng, shape, pieces, low, high):
    gain, own = 1.0, jax.random.fold_in(rng, 6)
    for dim, shards_of in pieces:
        steps = jnp.exp(jax.random.uniform(jax.random.fold_in(own, dim), (shards_of,), jnp.float32, low / len(pieces), high / len(pieces)))
        gain = gain * jnp.repeat(steps, shape[dim] // shards_of).reshape([-1 if axis == dim else 1 for axis in range(len(shape))])
    return gain


def cumulative_ranks(amount, lean):
    weights = [(1 << 20) // math.isqrt(standing ** lean) + 1 for standing in range(1, amount + 1)]
    scale = 1 + sum(weights) // (1 << 30)
    return np.cumsum(np.array([max(1, weight // scale) for weight in weights]))


def skewed_ids(own_key, extent, count, lean):
    table = cumulative_ranks(count, lean)
    lot = jax.random.randint(jax.random.fold_in(own_key, 1), extent, 0, int(table[count - 1]))
    rank = jnp.searchsorted(jnp.asarray(table, jnp.int32), lot, side="right")
    return jax.random.permutation(jax.random.fold_in(own_key, 2), count)[rank].astype(jnp.int32)


def centred(key, shape, scale, reach, shards=(), held_as=jnp.bfloat16):
    level = block_levels(key, shape, shards, -0.22, 0.18) if shards else 1.0
    array = jax.random.normal(key, shape, jnp.float32) * scale * level
    return jnp.minimum(jnp.maximum(array, -reach), reach).astype(held_as)


def setup_inputs(seed: int = 0) -> dict:
    streams_of = jax.random.split(jax.random.key(seed), 10)
    return {
        "g_real": centred(streams_of[0], (QSTEPS, NR, 2 * FV), NR ** -0.5, 0.1875, ((1, 32),)),
        "lattice": with_ends(jax.random.randint(streams_of[1], (3, NR), -20, 21), jax.random.fold_in(streams_of[1], 1), -20, 20).astype(jnp.int32),
        "u_rot": centred(streams_of[2], (2, NW, NW, KPTS), NW ** -0.5, 1.5, ((3, 128),), jnp.float32),
        "energy": jnp.clip(jax.random.uniform(streams_of[3], (NW, KPTS), jnp.float32, -2.0, 2.0) * block_levels(streams_of[3], (NW, KPTS), ((1, 128),), -0.4, 0.0), -2.0, 2.0),
        "band_mask": with_ends((jax.random.randint(streams_of[4], (NW, KPTS), 0, 4) < 3).astype(jnp.int32), jax.random.fold_in(streams_of[4], 1), 0, 1),
        "freq": jnp.clip(jnp.exp(jax.random.uniform(streams_of[5], (QSTEPS, MODES), jnp.float32, math.log(0.01), math.log(0.1))), 0.01, 0.1),
        "froh": centred(streams_of[6], (QSTEPS, 2, MODES), 1.0, 6.0, (), jnp.float32),
        "kq_index": jax.vmap(lambda own: jax.random.permutation(own, KDEV))(jax.random.split(streams_of[7], QSTEPS)).reshape((QSTEPS, KDEV)).astype(jnp.int32),
        "irr_id": with_ends(skewed_ids(streams_of[8], (KPTS,), IRR_GRP, 2), jax.random.fold_in(streams_of[8], 3), 0, IRR_GRP - 1).astype(jnp.int32),
    }


KT = 0.025
ETA = 0.05
TWO_PI = 2.0 * math.pi


def grid_points(first, count):
    index = first + jnp.arange(count, dtype=jnp.int32)
    return (index % NKM, (index // NKM) % NKM, (index // (NKM * NKM)) % NKM)


def phase_matrix(lattice_cols, grid):
    turns = lattice_cols[0][:, None] * grid[0][None, :] + lattice_cols[1][:, None] * grid[1][None, :]
    turns = jnp.mod(turns + lattice_cols[2][:, None] * grid[2][None, :], NKM)
    angle = turns.astype(jnp.float32) * (TWO_PI / NKM)
    cosine = jnp.cos(angle).astype(jnp.bfloat16)
    sine = jnp.sin(angle).astype(jnp.bfloat16)
    return jnp.stack([jnp.concatenate([cosine, sine], 1), jnp.concatenate([-sine, cosine], 1)])


def fourier(rows, phases):
    split = rows.reshape(rows.shape[0], 2, rows.shape[1] // 2).astype(jnp.float32)
    return lax.dot_general(split, phases.astype(jnp.float32), (((0, 1), (1, 0)), ((), ())),
                           precision=lax.Precision.HIGHEST, preferred_element_type=jnp.float32)


def contribution(vertex, own_rot, own_energy, far_rot, far_extra, freq_row, froh_row):
    modes = freq_row.shape[0]
    width = own_rot.shape[1]
    count = own_rot.shape[3]
    vertex_re = vertex[:, :count].reshape(modes, width, width, count)
    vertex_im = vertex[:, count:].reshape(modes, width, width, count)
    own_re, own_im = own_rot[0], own_rot[1]
    far_re, far_im = far_rot[0], far_rot[1]
    coup_re = froh_row[0][:, None, None, None]
    coup_im = froh_row[1][:, None, None, None]
    mixed_re = coup_re * own_re[None] - coup_im * own_im[None]
    mixed_im = coup_re * own_im[None] + coup_im * own_re[None]
    for inner in range(width):
        left_re = vertex_re[:, :, inner][:, :, None, :]
        left_im = vertex_im[:, :, inner][:, :, None, :]
        right_re = own_re[inner][None, None]
        right_im = own_im[inner][None, None]
        mixed_re = mixed_re + left_re * right_re - left_im * right_im
        mixed_im = mixed_im + left_re * right_im + left_im * right_re
    bloch_re = jnp.zeros((modes, width, width, count), jnp.float32)
    bloch_im = jnp.zeros((modes, width, width, count), jnp.float32)
    for inner in range(width):
        rot_re = far_re[inner][None, :, None, :]
        rot_im = far_im[inner][None, :, None, :]
        part_re = mixed_re[:, inner][:, None]
        part_im = mixed_im[:, inner][:, None]
        bloch_re = bloch_re + rot_re * part_re + rot_im * part_im
        bloch_im = bloch_im + rot_re * part_im - rot_im * part_re
    strength = (bloch_re * bloch_re + bloch_im * bloch_im) * far_extra[1][None, :, None, :]
    far_energy = far_extra[0]
    occupied = (1.0 / (jnp.exp(far_energy / KT) + 1.0))[None, :, None, :]
    bose = (1.0 / (jnp.exp(freq_row / KT) - 1.0))[:, None, None, None]
    phonon = freq_row[:, None, None, None]
    differ = own_energy[None, None, :, :] - far_energy[None, :, None, :]
    upper = differ + phonon
    lower = differ - phonon
    denom_up = upper * upper + ETA * ETA
    denom_low = lower * lower + ETA * ETA
    emission = bose + occupied
    absorb = bose + 1.0 - occupied
    real_part = strength * (emission * upper / denom_up + absorb * lower / denom_low)
    imag_part = -ETA * strength * (emission / denom_up + absorb / denom_low)
    return jnp.stack([real_part.sum((0, 1)), imag_part.sum((0, 1))])


def reference(g_real, lattice, u_rot, energy, band_mask, freq, froh, kq_index, irr_id):
    extra = jnp.stack([energy, band_mask.astype(jnp.float32)])
    weight = 1.0 / (QSTEPS * MODES * NW)
    blocks = N_GRP * N_KP

    def one_block(block):
        first = (block * KDEV).astype(jnp.int32)
        grid = grid_points(first, KDEV)
        phases = phase_matrix(lattice, grid)
        own_rot = lax.dynamic_slice_in_dim(u_rot, first, KDEV, 3)
        own_energy = lax.dynamic_slice_in_dim(energy, first, KDEV, 1)
        total = jnp.zeros((2, NW, KDEV), jnp.float32)
        for step in range(QSTEPS):
            vertex = fourier(g_real[step], phases)
            partner = ((block // N_KP + step + 1) % N_GRP) * N_KP + block % N_KP
            pstart = (partner * KDEV).astype(jnp.int32)
            order = kq_index[step]
            far_rot = jnp.take(lax.dynamic_slice_in_dim(u_rot, pstart, KDEV, 3), order, axis=3)
            far_extra = jnp.take(lax.dynamic_slice_in_dim(extra, pstart, KDEV, 2), order, axis=2)
            total = total + contribution(vertex, own_rot, own_energy, far_rot, far_extra, freq[step], froh[step])
        return total

    parts = lax.map(one_block, jnp.arange(blocks, dtype=jnp.int32))
    sigma_k = jnp.transpose(parts, (1, 2, 0, 3)).reshape(2, NW, KPTS) * weight
    global_id = ((jnp.arange(KPTS, dtype=jnp.int32) // KGRP) * IRR_GRP + irr_id).astype(jnp.int32)
    flat = sigma_k.reshape(2 * NW, KPTS).T
    sums = jax.ops.segment_sum(flat, global_id, num_segments=IRR)
    counts = jax.ops.segment_sum(jnp.ones((KPTS,), jnp.float32), global_id, num_segments=IRR)
    sigma_irr = (sums / jnp.maximum(counts, 1.0)[:, None]).T.reshape(2, NW, IRR)
    return sigma_k, sigma_irr
```

```python
import math
import jax
import jax.numpy as jnp
from jax import lax
from jax.experimental import pallas as pl
from jax.experimental.pallas import tpu as pltpu
from jax.sharding import PartitionSpec as P

KT = 0.025
ETA = 0.05
NKM = 40
F32, BF16 = jnp.float32, jnp.bfloat16
NT = (((1,), (1,)), ((), ()))


def mod_mesh(values):
    return values - NKM * jnp.floor((values + 0.5) * (1.0 / NKM))


def turn(steps):
    x = (steps - 20.0) * (1.0 / 20.0)
    y = x * x
    pi2 = math.pi * math.pi
    cos, sin = 0.0, 0.0
    for n in range(8, -1, -1):
        cos = cos * y + (-1.0) ** n * math.pi ** (2 * n) / math.factorial(2 * n)
        sin = sin * y + (-1.0) ** n * math.pi ** (2 * n + 1) / math.factorial(2 * n + 1)
    return -cos, -(sin * x)


def swap_bits(parts, width, masks):
    parts = list(parts)
    span = len(parts)
    bit = 1
    while bit < span:
        mask = masks[bit * width]
        for low in range(span):
            if low & bit:
                continue
            a, b = parts[low], parts[low | bit]
            parts[low] = jnp.where(mask, pltpu.roll(b, bit * width, 1), a)
            parts[low | bit] = jnp.where(mask, b, pltpu.roll(a, 128 - bit * width, 1))
        bit *= 2
    return parts


def pieces(x, count):
    out = []
    for _ in range(count):
        head = x.astype(BF16)
        out.append(head)
        x = x - head.astype(F32)
    return out


def dot(a, b):
    return jnp.dot(a, b, preferred_element_type=F32)


def dot_nt(a, b):
    return lax.dot_general(a, b, NT, preferred_element_type=F32)


def compute_kernel(where, g_ref, u_ref, e_ref, lat_ref, kq_ref, freq_ref, froh_ref, out_ref,
                   ac, as_, bc, bs, ph, vs, yk, xs, t1, t2, ex, fa, sums, rep, diag, perm):
    zh0, g0, bases = where(froh_ref)
    step = zh0
    mode0 = g0 * 3
    lane = lax.broadcasted_iota(jnp.int32, (8, 128), 1)
    masks = {s: (lane & s) != 0 for s in (1, 2, 4, 8, 16, 32, 64)}

    lat = lat_ref[...].astype(F32)
    n1 = lax.broadcasted_iota(jnp.int32, (40, 1024), 0).astype(F32)
    ac[...], as_[...] = turn(mod_mesh(n1 * lat[0:1]))
    row16 = lax.broadcasted_iota(jnp.int32, (16, 1024), 0).astype(F32)
    for s in range(8):
        i0 = row16 * 8.0 + bases[s].astype(F32)
        q2 = jnp.floor((i0 + 0.5) * (1.0 / 40.0))
        n2 = mod_mesh(q2)
        n3 = mod_mesh(jnp.floor((i0 + 0.5) * (1.0 / 1600.0)))
        bc[16 * s:16 * s + 16], bs[16 * s:16 * s + 16] = turn(mod_mesh(n2 * lat[1:2] + n3 * lat[2:3]))
    rr = lax.broadcasted_iota(jnp.int32, (128, 2048), 0)
    rl = lax.broadcasted_iota(jnp.int32, (128, 2048), 1)
    rep[...] = jnp.where(rl // 16 == rr, 1.0, 0.0).astype(BF16)
    sr = lax.broadcasted_iota(jnp.int32, (128, 128), 0)
    sl = lax.broadcasted_iota(jnp.int32, (128, 128), 1)
    diag[...] = jnp.where(sr // 16 == sl // 16, 1.0, 0.0).astype(BF16)
    eye = jnp.where(sr == sl, 1.0, 0.0).astype(BF16)
    order = kq_ref[pl.ds(step, 1), :]
    onehot = jnp.where(sr == order, 1.0, 0.0)
    perm[...] = onehot.T.astype(BF16)
    lanes768 = lax.broadcasted_iota(jnp.int32, (1, 256), 1)
    onsite = jnp.where(lanes768 // 16 == lanes768 % 16, 1.0, 0.0)
    fro = [jnp.concatenate([onsite * froh_ref[step, c, mode0 + m] for m in range(3)], 1) for c in range(2)]

    for s in range(8):
        own = pieces(e_ref[s, 0:16], 3)
        far = (s // 4) * 4 + lax.rem(s % 4 + step + 1, 4)
        far_e = pieces(e_ref[far, 0:16], 3) + [e_ref[far, 16:32].astype(BF16)]
        moved = dot_nt(jnp.concatenate(far_e, 0), perm[...]).astype(BF16)
        both = dot(jnp.concatenate(own + [moved], 0), rep[...])
        ex[s * 16:s * 16 + 16] = both[0:16] + both[16:32] + both[32:48]
        fe = both[48:64] + both[64:80] + both[80:96]
        fm = both[96:112]
        r16 = lax.broadcasted_iota(jnp.int32, (16, 2048), 0)
        l16 = lax.broadcasted_iota(jnp.int32, (16, 2048), 1) % 16
        pick = r16 == l16
        fe = jnp.where(pick, fe, 0.0).sum(0, keepdims=True)
        fm = jnp.where(pick, fm, 0.0).sum(0, keepdims=True)
        fa[s * 8:s * 8 + 1] = fe
        fa[s * 8 + 1:s * 8 + 2] = fm
        fa[s * 8 + 2:s * 8 + 3] = 1.0 / (jnp.exp(fe * (1.0 / KT)) + 1.0)

    bose, phonon = [], []
    for m in range(3):
        w = jnp.full((1, 128), freq_ref[step, mode0 + m], F32)
        phonon.append(w)
        bose.append(1.0 / (jnp.exp(w / KT) - 1.0))

    def blocks(src, c):
        for hi in range(2):
            for half in range(2):
                col = c * 2 + hi
                parts = [src[col, pl.ds(half * 64 + k, 8, stride=8), :] for k in range(8)]
                parts = swap_bits(parts, 16, masks)
                yield hi, half, parts

    def one_set(s, carry):
        base = bases_at(s)
        def pair(o2, carry2):
            cs, sn = [], []
            for h in range(2):
                o = o2 * 2 + h
                start = pl.multiple_of(lax.rem(base + o * 8, NKM), 8)
                a_c, a_s = ac[pl.ds(start, 8)], as_[pl.ds(start, 8)]
                b_c, b_s = bc[pl.ds(s * 16 + o, 1)], bs[pl.ds(s * 16 + o, 1)]
                cs.append(a_c * b_c - a_s * b_s)
                sn.append(a_s * b_c + a_c * b_s)
            co = jnp.concatenate(cs, 0).astype(BF16)
            si = jnp.concatenate(sn, 0).astype(BF16)
            at = pl.multiple_of(o2 * 16, 16)
            ph[pl.ds(at, 16), 0:1024] = co
            ph[pl.ds(at, 16), 1024:2048] = -si
            at = pl.multiple_of(o2 * 16 + 128, 16)
            ph[pl.ds(at, 16), 0:1024] = si
            ph[pl.ds(at, 16), 1024:2048] = co
            return carry2
        lax.fori_loop(0, 8, pair, 0)
        for c in range(2):
            ver = dot(ph[c * 128:c * 128 + 128], g_ref[...]) + fro[c]
            for tile in range(6):
                vs[c * 6 + tile] = ver[:, tile * 128:tile * 128 + 128]
        far = (s // 4) * 4 + lax.rem(lax.rem(s, 4) + step + 1, 4)
        for w, left, at in ((0, eye, s), (1, perm[...], far)):
            turned = dot_nt(left, u_ref[at])
            for tile in range(4):
                yk[tile] = turned[:, tile * 128:tile * 128 + 128]
            for c in range(2):
                for hi, half, parts in blocks(yk, c):
                    for b in range(8):
                        xs[w * 2 + c, pl.ds(half * 128 + hi * 8 + b, 8, stride=16), :] = parts[b]
        for c in range(2):
            for m in range(3):
                for hi in range(2):
                    for half in range(2):
                        col = c * 6 + m * 2 + hi
                        parts = [vs[col, pl.ds(half * 64 + k, 8, stride=8), :] for k in range(8)]
                        parts = swap_bits(parts, 16, masks)
                        for a in range(8):
                            t1[c, pl.ds(half * 384 + m * 16 + hi * 8 + a, 8, stride=48), :] = parts[a]

        def rows_of(ref, o):
            rows = slice(o * 48, o * 48 + 48)
            return jnp.concatenate([ref[0, rows], ref[1, rows]], 1).astype(BF16)

        def block_matrix(w, o, sign):
            xr = xs[w * 2, o * 16:o * 16 + 16].astype(BF16)
            xi = xs[w * 2 + 1, o * 16:o * 16 + 16].astype(BF16)
            d = diag[...]
            wr = jnp.concatenate([xr] * 8, 0) * d
            wi = jnp.concatenate([xi] * 8, 0) * d
            wn = jnp.concatenate([-xi] * 8, 0) * d
            if sign > 0:
                return jnp.concatenate([jnp.concatenate([wr, wi], 1), jnp.concatenate([wn, wr], 1)], 0)
            return jnp.concatenate([jnp.concatenate([wr, wn], 1), jnp.concatenate([wi, wr], 1)], 0)

        for o in range(16):
            mixed = dot(rows_of(t1, o), block_matrix(0, o, 1))
            t2[0, o * 48:o * 48 + 48] = mixed[:, 0:128]
            t2[1, o * 48:o * 48 + 48] = mixed[:, 128:256]
        for c in range(2):
            for m in range(3):
                for half in range(2):
                    at = half * 384 + m * 16
                    parts = [t2[c, pl.ds(at + a, 8, stride=48), :] for a in range(16)]
                    parts = swap_bits(parts, 1, masks)
                    for n in range(16):
                        t1[c, pl.ds(at + n, 8, stride=48), :] = parts[n]
        for o in range(16):
            bl = dot(rows_of(t1, o), block_matrix(1, o, -1))
            br, bi = bl[:, 0:128], bl[:, 128:256]
            strength = br * br + bi * bi
            cols = slice(o * 128, o * 128 + 128)
            eo = ex[pl.ds(pl.multiple_of(s * 16, 16), 16), cols]
            rows = fa[pl.ds(pl.multiple_of(s * 8, 8), 8), cols]
            fe, fm, occ = rows[0:1], rows[1:2], rows[2:3]
            diff = eo - fe
            re, im = 0.0, 0.0
            for m in range(3):
                em = fm * (bose[m] + occ)
                ab = fm * (bose[m] + 1.0 - occ)
                up = diff + phonon[m]
                lo = diff - phonon[m]
                du = up * up + ETA * ETA
                dl = lo * lo + ETA * ETA
                scale = strength[m * 16:m * 16 + 16] / (du * dl)
                e1 = em * dl
                a1 = ab * du
                re = re + scale * (e1 * up + a1 * lo)
                im = im + scale * (e1 + a1)
            sums[pl.ds(pl.multiple_of(s * 32, 32), 16), cols] = re
            sums[pl.ds(pl.multiple_of(s * 32 + 16, 16), 16), cols] = im * (-ETA)
        return carry

    def bases_at(s):
        return bases[0] + lax.rem(s, 4) * 4096 + (s // 4) * 512

    lax.fori_loop(0, 8, one_set, 0)
    hi, lo = pieces(sums[...], 2)
    out_ref[...] = (dot_nt(hi, rep[...]) + dot_nt(lo, rep[...])) * (1.0 / 384.0)


def compute(where, g, u, e, lat, kq, freq, froh):
    vm = pl.BlockSpec(memory_space=pltpu.VMEM)
    sm = pl.BlockSpec(memory_space=pltpu.SMEM)
    return pl.pallas_call(
        lambda *refs: compute_kernel(where, *refs),
        out_shape=jax.ShapeDtypeStruct((256, 128), F32),
        in_specs=[vm, vm, vm, vm, vm, sm, sm],
        out_specs=vm,
        scratch_shapes=[
            pltpu.VMEM((40, 1024), F32), pltpu.VMEM((40, 1024), F32),
            pltpu.VMEM((128, 1024), F32), pltpu.VMEM((128, 1024), F32),
            pltpu.VMEM((256, 2048), BF16),
            pltpu.VMEM((12, 128, 128), F32),
            pltpu.VMEM((4, 128, 128), F32),
            pltpu.VMEM((4, 256, 128), F32),
            pltpu.VMEM((2, 768, 128), F32), pltpu.VMEM((2, 768, 128), F32),
            pltpu.VMEM((128, 2048), F32), pltpu.VMEM((64, 2048), F32),
            pltpu.VMEM((256, 2048), F32),
            pltpu.VMEM((128, 2048), BF16), pltpu.VMEM((128, 128), BF16), pltpu.VMEM((128, 128), BF16),
        ],
        compiler_params=pltpu.CompilerParams(vmem_limit_bytes=50 * 2 ** 20),
    )(g, u, e, lat, kq, freq, froh)


MESH = pl.DeviceIdType.MESH


def position():
    kp = lax.axis_index("kp")
    return lax.axis_index("grp"), kp // 8, kp // 4 % 2, kp % 4


def at(g, x, zh, y):
    return (g, x * 8 + zh * 4 + y)


def column(g, zh):
    for hop in range(1, 8):
        other = (zh * 4 + g + hop) % 8
        yield hop, other % 4, other // 4


def greet(devices):
    barrier = pltpu.get_barrier_semaphore()
    for device in devices:
        pl.semaphore_signal(barrier, inc=1, device_id=device, device_id_type=MESH)
    pl.semaphore_wait(barrier, len(devices))


def gather_kernel(g_ref, u_ref, en_ref, mask_ref, gbuf, ubuf, ebuf,
                  local_sem, z_send, z_recv, u_send, u_recv, e_send, e_recv, g_send, g_recv):
    g, x, zh, y = position()
    mine = zh * 4 + g
    others = [at(g2, x, zh2, y) for _, g2, zh2 in column(g, zh)]
    for hop in range(1, 4):
        others.append(at(g, (x + hop) % 4, zh, y))
        others.append(at(g, x, zh, (y + hop) % 4))
    greet(others)

    def remote(src, dst, send, recv, device):
        return pltpu.make_async_remote_copy(src_ref=src, dst_ref=dst, send_sem=send, recv_sem=recv,
                                            device_id=device, device_id_type=MESH)

    def part(step, triple, c):
        return g_ref.at[step, :, pl.ds(pl.multiple_of(c * 3072 + triple * 768, 768), 768)]

    pz, pg = 1 - zh, (g + 2) % 4
    first = []
    for c in range(2):
        far = remote(part(pz, pg, c), gbuf.at[c, x, zh, y], z_send.at[c], z_recv.at[c], at(pg, x, pz, y))
        far.start()
        near = pltpu.make_async_copy(part(zh, g, c), gbuf.at[c, x, zh, y], local_sem.at[c])
        near.start()
        first.append((far, near))
    ubuf[mine] = u_ref[...].astype(BF16)
    ebuf[mine, 0:16] = en_ref[...]
    ebuf[mine, 16:32] = mask_ref[...].astype(F32)
    small = []
    for hop, g2, zh2 in column(g, zh):
        small.append(remote(ubuf.at[mine], ubuf.at[mine], u_send.at[hop], u_recv.at[hop], at(g2, x, zh2, y)))
        small.append(remote(ebuf.at[mine], ebuf.at[mine], e_send.at[hop], e_recv.at[hop], at(g2, x, zh2, y)))
    sent = []

    def to_x(c, ys, hop, sem):
        piece = gbuf.at[c, x, :, ys]
        copy = remote(piece, piece, g_send.at[c, sem], g_recv.at[c, sem], at(g, (x + hop) % 4, zh, y))
        copy.start()
        sent.append(copy)

    def to_y(c, xs, hop, sem):
        piece = gbuf.at[c, xs, :, y]
        copy = remote(piece, piece, g_send.at[c, sem], g_recv.at[c, sem], at(g, x, zh, (y + hop) % 4))
        copy.start()
        sent.append(copy)

    for far, near in first:
        near.wait()
        far.wait()
    for hop in (1, 3, 2):
        to_x(0, y, hop, 16 + hop)
        to_y(1, x, hop, 16 + hop)
    for copy in small:
        copy.start()
    for hop in (1, 3, 2):
        to_y(0, x, hop, hop)
        to_x(1, y, hop, hop)
    for hop in (1, 3, 2):
        xs, ys = (x + 4 - hop) % 4, (y + 4 - hop) % 4
        got = gbuf.at[0, xs, :, y]
        remote(got, got, g_send.at[0, 16 + hop], g_recv.at[0, 16 + hop], at(g, xs, zh, y)).wait_recv()
        for to in (1, 3, 2):
            to_y(0, xs, to, 4 * hop + to)
        got = gbuf.at[1, x, :, ys]
        remote(got, got, g_send.at[1, 16 + hop], g_recv.at[1, 16 + hop], at(g, x, zh, ys)).wait_recv()
        for to in (1, 3, 2):
            to_x(1, ys, to, 4 * hop + to)
    for copy in small:
        copy.wait()
    for hop in (0, 1, 3, 2):
        for to in (1, 3, 2):
            xs, ys = (x + 4 - hop) % 4, (y + 4 - to) % 4
            got = gbuf.at[0, xs, :, ys]
            remote(got, got, g_send.at[0, 0], g_recv.at[0, 4 * hop + to], at(g, x, zh, ys)).wait_recv()
            xs, ys = (x + 4 - to) % 4, (y + 4 - hop) % 4
            got = gbuf.at[1, xs, :, ys]
            remote(got, got, g_send.at[1, 0], g_recv.at[1, 4 * hop + to], at(g, xs, zh, y)).wait_recv()
    for copy in sent:
        copy.wait_send()


def gather(g_real, u, energy, mask):
    vm = pl.BlockSpec(memory_space=pltpu.VMEM)
    anywhere = pl.BlockSpec(memory_space=pl.ANY)
    dma = pltpu.SemaphoreType.DMA
    return pl.pallas_call(
        gather_kernel,
        out_shape=(jax.ShapeDtypeStruct((2, 4, 2, 4, 32, 768), BF16),
                   jax.ShapeDtypeStruct((8, 512, 128), BF16),
                   jax.ShapeDtypeStruct((8, 32, 128), F32)),
        in_specs=[anywhere, vm, vm, vm],
        out_specs=(vm, vm, vm),
        scratch_shapes=[dma((2,)), dma((2,)), dma((2,)), dma((8,)), dma((8,)), dma((8,)), dma((8,)),
                        dma((2, 20)), dma((2, 20))],
        compiler_params=pltpu.CompilerParams(collective_id=0, has_side_effects=True,
                                             vmem_limit_bytes=40 * 2 ** 20),
    )(g_real, u, energy, mask)


def reduce_kernel(part_ref, irr_ref, sigma_ref, star_ref, got, stars, blocks,
                  a_send, a_recv, b_send, b_recv):
    g, x, zh, y = position()
    me = x * 8 + zh * 4 + y
    mine = zh * 4 + g
    others = [at(g2, x, zh2, y) for _, g2, zh2 in column(g, zh)]
    greet(others + [(g, (me + hop) % 32) for hop in range(1, 32)])
    copies = []
    for hop, g2, zh2 in column(g, zh):
        owner = zh2 * 4 + g2
        copies.append(pltpu.make_async_remote_copy(
            src_ref=part_ref.at[owner], dst_ref=got.at[hop], send_sem=a_send.at[hop],
            recv_sem=a_recv.at[hop], device_id=at(g2, x, zh2, y), device_id_type=MESH))
        copies[-1].start()
    labels = lax.broadcasted_iota(jnp.int32, (512, 128), 0)
    member = jnp.where(labels == irr_ref[...], 1.0, 0.0).astype(BF16)
    total = part_ref[mine]
    for hop, copy in enumerate(copies, 1):
        copy.wait_recv()
        total = total + got[hop]
    sigma_ref[...] = total
    columns = jnp.concatenate(pieces(total, 3) + [jnp.ones((32, 128), BF16)], 0)
    stars[...] = dot_nt(member, columns)
    for hop in range(1, 32):
        owner = (me + hop) % 32
        copies.append(pltpu.make_async_remote_copy(
            src_ref=stars.at[pl.ds(pl.multiple_of(owner * 16, 16), 16)], dst_ref=blocks.at[hop],
            send_sem=b_send.at[hop], recv_sem=b_recv.at[hop], device_id=(g, owner), device_id_type=MESH))
        copies[-1].start()
    mean = stars[pl.ds(pl.multiple_of(me * 16, 16), 16)]
    for hop in range(1, 32):
        copies[6 + hop].wait_recv()
        mean = mean + blocks[hop]
    count = pltpu.roll(mean, 32, 1)
    mean = mean + pltpu.roll(mean, 96, 1) + pltpu.roll(mean, 64, 1)
    star_ref[...] = mean / jnp.maximum(count, 1.0)
    for copy in copies:
        copy.wait_send()


def reduce(part, irr):
    vm = pl.BlockSpec(memory_space=pltpu.VMEM)
    dma = pltpu.SemaphoreType.DMA
    return pl.pallas_call(
        reduce_kernel,
        out_shape=(jax.ShapeDtypeStruct((32, 128), F32), jax.ShapeDtypeStruct((16, 128), F32)),
        in_specs=[vm, vm],
        out_specs=(vm, vm),
        scratch_shapes=[pltpu.VMEM((8, 32, 128), F32), pltpu.VMEM((512, 128), F32),
                        pltpu.VMEM((32, 16, 128), F32),
                        dma((8,)), dma((8,)), dma((32,)), dma((32,))],
        compiler_params=pltpu.CompilerParams(collective_id=1, has_side_effects=True),
    )(part, irr)


def local(g_real, lattice, u_rot, energy, band_mask, freq, froh, kq_index, irr_id):
    def where(_):
        g, x, zh, y = position()
        first = (x * 8 + y) * 128
        return zh, g, [first + s % 4 * 4096 + s // 4 * 512 for s in range(8)]

    vertex, rotations, levels = gather(g_real, u_rot.reshape(512, 128), energy, band_mask)
    part = compute(where, vertex.reshape(2048, 768), rotations, levels, lattice, kq_index, freq, froh)
    sigma, star = reduce(part.reshape(8, 32, 128), irr_id.reshape(1, 128))
    return sigma.reshape(2, 16, 128), star[:, :32].T.reshape(2, 16, 16)


def solution(mesh):
    in_specs = (
        P(None, "kp", None),
        P(),
        P(None, None, None, ("grp", "kp")),
        P(None, ("grp", "kp")),
        P(None, ("grp", "kp")),
        P(),
        P(),
        P(),
        P(("grp", "kp")),
    )
    out_specs = (P(None, None, ("grp", "kp")), P(None, None, ("grp", "kp")))
    return jax.shard_map(local, mesh=mesh, in_specs=in_specs, out_specs=out_specs, check_vma=False)
```

```python
import functools
import math
from types import SimpleNamespace

import jax
import jax.numpy as jnp
from jax import lax
from jax.experimental import pallas as pl
from jax.experimental.pallas import tpu as pltpu
from jax.sharding import PartitionSpec as P

KT = 0.025
ETA = 0.05
NKM = 40
F32, BF16 = jnp.float32, jnp.bfloat16
NT = (((1,), (1,)), ((), ()))
MESH = pl.DeviceIdType.MESH


def mod_mesh(values):
    return values - NKM * jnp.floor((values + 0.5) * (1.0 / NKM))


def turn(steps):
    x = (steps - 20.0) * (1.0 / 20.0)
    y = x * x
    cos, sin = 0.0, 0.0
    for n in range(8, -1, -1):
        cos = cos * y + (-1.0) ** n * math.pi ** (2 * n) / math.factorial(2 * n)
        sin = sin * y + (-1.0) ** n * math.pi ** (2 * n + 1) / math.factorial(2 * n + 1)
    return -cos, -(sin * x)


def pieces(x, count):
    out = []
    for _ in range(count):
        head = x.astype(BF16)
        out.append(head)
        x = x - head.astype(F32)
    return out


def dot(a, b):
    return jnp.dot(a, b, preferred_element_type=F32)


def dot_nt(a, b):
    return lax.dot_general(a, b, NT, preferred_element_type=F32)


def iota(shape, axis):
    return lax.broadcasted_iota(jnp.int32, shape, axis)


def swap_groups(parts):
    parts = list(parts)
    lane = iota(parts[0].shape, 1)
    for bit in (1, 2, 4):
        mask = (lane & (16 * bit)) != 0
        for low in range(8):
            if low & bit == 0:
                a, b = parts[low], parts[low | bit]
                parts[low] = jnp.where(mask, pltpu.roll(b, 16 * bit, 1), a)
                parts[low | bit] = jnp.where(mask, b, pltpu.roll(a, 128 - 16 * bit, 1))
    return parts


def scratch_shapes():
    vm = pltpu.VMEM
    return dict(
        g=vm((3, 2, 4, 2, 4, 32, 256), BF16),
        u=vm((8, 512, 128), BF16),
        e=vm((8, 32, 128), F32),
        ac=vm((40, 1024), F32), as_=vm((40, 1024), F32),
        bc=vm((128, 1024), F32), bs=vm((128, 1024), F32),
        ph=vm((8, 256, 2048), BF16),
        v=vm((2, 1024, 256), BF16),
        xs=vm((2, 8, 3, 256, 128), BF16),
        t1=vm((8, 3, 256, 256), BF16),
        t2=vm((6, 128, 256), BF16),
        t3=vm((6, 256, 128), BF16),
        ex=vm((128, 2048), F32), fa=vm((64, 2048), F32),
        sums=vm((256, 2048), F32),
        rep=vm((128, 2048), BF16), diag=vm((128, 128), BF16), eye=vm((256, 256), BF16),
        mix=vm((256, 256), BF16), perm=vm((128, 128), BF16), turned=vm((128, 128), BF16),
    )


def constants(r):
    rr, rl = iota((128, 2048), 0), iota((128, 2048), 1)
    r.rep[...] = jnp.where(rl // 16 == rr, 1.0, 0.0).astype(BF16)
    sr, sl = iota((128, 128), 0), iota((128, 128), 1)
    r.diag[...] = jnp.where(sr // 16 == sl // 16, 1.0, 0.0).astype(BF16)
    br, bl = iota((256, 256), 0), iota((256, 256), 1)
    r.eye[...] = jnp.where(br == bl, 1.0, 0.0).astype(BF16)
    r.mix[...] = jnp.where((br // 16 == bl % 16) & (br % 16 == bl // 16), 1.0, 0.0).astype(BF16)


def partner_order(r, kq, step):
    sr, sl = iota((128, 128), 0), iota((128, 128), 1)
    order = jnp.where(step == 0, kq[0:1, :], kq[1:2, :])
    perm = jnp.where(sr == order, 1.0, 0.0).T.astype(BF16)
    r.perm[...] = perm
    regroup = jnp.where((sr // 16 == sl % 8) & (sr % 16 == sl // 8), 1.0, 0.0).astype(BF16)
    r.turned[...] = dot(regroup, perm).astype(BF16)


def tables(r, lattice, first):
    lat = lattice.astype(F32)
    r.ac[...], r.as_[...] = turn(mod_mesh(iota((40, 1024), 0).astype(F32) * lat[0:1]))
    row16 = iota((16, 1024), 0).astype(F32)

    def one(s, carry):
        i0 = row16 * 8.0 + first(s).astype(F32) + 0.5
        n2 = mod_mesh(jnp.floor(i0 * (1.0 / 40.0)))
        n3 = mod_mesh(jnp.floor(i0 * (1.0 / 1600.0)))
        rows = pl.ds(pl.multiple_of(s * 16, 16), 16)
        r.bc[rows], r.bs[rows] = turn(mod_mesh(n2 * lat[1:2] + n3 * lat[2:3]))
        return carry

    lax.fori_loop(0, 8, one, 0)


def phases(r, s, first):
    base = first(s)

    def pair(o2, carry):
        cs, sn = [], []
        for h in range(2):
            o = o2 * 2 + h
            rows = pl.ds(pl.multiple_of(lax.rem(base + o * 8, NKM), 8), 8)
            a_c, a_s = r.ac[rows], r.as_[rows]
            b_c, b_s = r.bc[pl.ds(s * 16 + o, 1)], r.bs[pl.ds(s * 16 + o, 1)]
            cs.append(a_c * b_c - a_s * b_s)
            sn.append(a_s * b_c + a_c * b_s)
        co = jnp.concatenate(cs, 0).astype(BF16)
        si = jnp.concatenate(sn, 0)
        up = pl.ds(pl.multiple_of(o2 * 16, 16), 16)
        low = pl.ds(pl.multiple_of(o2 * 16 + 128, 16), 16)
        r.ph[s, up, 0:1024] = co
        r.ph[s, up, 1024:2048] = (-si).astype(BF16)
        r.ph[s, low, 0:1024] = si.astype(BF16)
        r.ph[s, low, 1024:2048] = co
        return carry

    lax.fori_loop(0, 8, pair, 0)


def partner_set(s, step):
    return s // 4 * 4 + lax.rem(lax.rem(s, 4) + step + 1, 4)


def levels(r, s, step):
    own = pieces(r.e[s, 0:16], 3)
    far = partner_set(s, step)
    far_e = pieces(r.e[far, 0:16], 3) + [r.e[far, 16:32].astype(BF16)]
    moved = dot_nt(jnp.concatenate(far_e, 0), r.perm[...]).astype(BF16)
    both = dot(jnp.concatenate(own + [moved], 0), r.rep[...])
    r.ex[pl.ds(pl.multiple_of(s * 16, 16), 16)] = both[0:16] + both[16:32] + both[32:48]
    pick = iota((16, 2048), 0) == iota((16, 2048), 1) % 16
    fe = jnp.where(pick, both[48:64] + both[64:80] + both[80:96], 0.0).sum(0, keepdims=True)
    fm = jnp.where(pick, both[96:112], 0.0).sum(0, keepdims=True)
    occ = 1.0 / (jnp.exp(fe * (1.0 / KT)) + 1.0)
    r.fa[pl.ds(pl.multiple_of(s * 8, 8), 8)] = jnp.concatenate([fe, fm, occ, jnp.zeros((5, 2048), F32)], 0)


def regroup_rows(r, tiles):
    cols = []
    for c in range(2):
        rows = []
        for hi in range(2):
            t = tiles[c][hi]
            rows += swap_groups([t[k * 16:k * 16 + 16] for k in range(8)])
        cols.append(jnp.concatenate(rows, 0))
    return dot(r.mix[...], jnp.concatenate(cols, 1)).astype(BF16)


def rotations(r, s, step):
    for w, left, at in ((0, r.eye[0:128, 0:128], s), (1, r.turned[...], partner_set(s, step))):
        points = dot_nt(left, r.u[at]).astype(BF16)
        out = regroup_rows(r, [[points[:, c * 256 + hi * 128:c * 256 + hi * 128 + 128] for hi in range(2)]
                               for c in range(2)])
        r.xs[w, s, 0] = out[:, 0:128]
        r.xs[w, s, 1] = out[:, 128:256]
        r.xs[w, s, 2] = -out[:, 128:256]


def vertex(r, m, half, onsite):
    rows = r.ph[half * 4:half * 4 + 4].reshape(1024, 2048)
    v = dot(rows, r.g[m].reshape(2048, 256))
    for s in range(4):
        for c in range(2):
            at = s * 256 + c * 128
            r.v[half, at:at + 128] = (v[at:at + 128] + onsite[c]).astype(BF16)


def regroup_vertex(r, m, half):
    for s in range(4):
        parts = [[r.v[half, s * 256 + c * 128:s * 256 + c * 128 + 128, hi * 128:hi * 128 + 128] for hi in range(2)]
                 for c in range(2)]
        r.t1[half * 4 + s, m] = regroup_rows(r, parts)


def block_matrix(r, w, s, o, sign):
    rows = slice(o * 16, o * 16 + 16)
    d = r.diag[...]
    wr, wi, wn = [jnp.concatenate([r.xs[w, s, i, rows]] * 8, 0) * d for i in range(3)]
    if sign > 0:
        return jnp.concatenate([jnp.concatenate([wr, wi], 1), jnp.concatenate([wn, wr], 1)], 0)
    return jnp.concatenate([jnp.concatenate([wr, wn], 1), jnp.concatenate([wi, wr], 1)], 0)


def self_energy(r, s, bose, phonon):
    for o in range(16):
        rows = slice(o * 16, o * 16 + 16)
        left = jnp.concatenate([r.t1[s, m, rows] for m in range(3)], 0)
        mixed = dot(left, block_matrix(r, 0, s, o, 1)).astype(BF16)
        inner = slice(o % 8 * 16, o % 8 * 16 + 16)
        for m in range(3):
            r.t2[o // 8 * 3 + m, inner] = mixed[m * 16:m * 16 + 16]
    for i in range(6):
        r.t3[i] = dot_nt(r.eye[...], r.t2[i]).astype(BF16)
    for o in range(16):
        hi, lo = o // 2, o % 2
        left = jnp.concatenate(
            [jnp.concatenate([r.t3[lo * 3 + m, c * 128 + hi * 16:c * 128 + hi * 16 + 16] for c in range(2)], 1)
             for m in range(3)], 0)
        bloch = dot(left, block_matrix(r, 1, s, o, -1))
        br, bi = bloch[:, 0:128], bloch[:, 128:256]
        strength = br * br + bi * bi
        cols = slice(o * 128, o * 128 + 128)
        eo = r.ex[pl.ds(pl.multiple_of(s * 16, 16), 16), cols]
        far = r.fa[pl.ds(pl.multiple_of(s * 8, 8), 8), cols]
        fe, fm, occ = far[0:1], far[1:2], far[2:3]
        diff = eo - fe
        re, im = 0.0, 0.0
        for m in range(3):
            em = fm * (bose[m] + occ)
            ab = fm * (bose[m] + 1.0 - occ)
            up = diff + phonon[m]
            lw = diff - phonon[m]
            du = up * up + ETA * ETA
            dl = lw * lw + ETA * ETA
            scale = strength[m * 16:m * 16 + 16] / (du * dl)
            e1 = em * dl
            a1 = ab * du
            re = re + scale * (e1 * up + a1 * lw)
            im = im + scale * (e1 + a1)
        r.sums[pl.ds(pl.multiple_of(s * 32, 32), 16), cols] = re
        r.sums[pl.ds(pl.multiple_of(s * 32 + 16, 16), 16), cols] = im * (-ETA)


def band_sum(r):
    hi, lo = pieces(r.sums[...], 2)
    return (dot_nt(hi, r.rep[...]) + dot_nt(lo, r.rep[...])) * (1.0 / 384.0)


def mode_terms(freq, froh, step, mode0):
    lane = iota((1, 256), 1)
    site = jnp.where(lane // 16 == lane % 16, 1.0, 0.0)
    onsite = [[site * froh[step, c, mode0 + m] for c in range(2)] for m in range(3)]
    phonon = [jnp.full((1, 128), freq[step, mode0 + m], F32) for m in range(3)]
    bose = [1.0 / (jnp.exp(w * (1.0 / KT)) - 1.0) for w in phonon]
    return onsite, phonon, bose


def loop(body):
    def step(s, carry):
        body(s)
        return carry
    lax.fori_loop(0, 8, step, 0)


def position():
    kp = lax.axis_index("kp")
    return lax.axis_index("grp"), kp // 8, kp // 4 % 2, kp % 4


def at(g, x, zh, y):
    return (g, x * 8 + zh * 4 + y)


def column(g, zh):
    for hop in range(1, 8):
        other = (zh * 4 + g + hop) % 8
        yield hop, other % 4, other // 4


def remote(src, dst, send, recv, device):
    return pltpu.make_async_remote_copy(src_ref=src, dst_ref=dst, send_sem=send, recv_sem=recv,
                                        device_id=device, device_id_type=MESH)


def semaphores():
    dma = pltpu.SemaphoreType.DMA
    return dict(
        in_sem=dma((6,)), near_sem=dma((2, 3)),
        z_send=dma((2, 3)), z_recv=dma((2, 3)),
        u_send=dma((8,)), u_recv=dma((8,)), e_send=dma((8,)), e_recv=dma((8,)),
        p_send=dma((2, 2, 4)), p_recv=dma((2, 2, 4)),
        g_send=dma((2, 3, 16)), g_recv=dma((2, 3, 16)),
        a_send=dma((8,)), a_recv=dma((8,)), b_send=dma((32,)), b_recv=dma((32,)),
    )


def io_shapes():
    vm = pltpu.VMEM
    return dict(
        uin=vm((512, 128), F32), en=vm((16, 128), F32), mask=vm((16, 128), jnp.int32),
        lat=vm((3, 1024), jnp.int32), kq=vm((2, 128), jnp.int32), irr=vm((1, 128), jnp.int32),
        part=vm((8, 32, 128), F32), got=vm((8, 32, 128), F32),
        stars=vm((512, 128), F32), blocks=vm((32, 16, 128), F32),
    )


def kernel(names, g_ref, u_ref, en_ref, mask_ref, lat_ref, kq_ref, irr_ref, freq, froh,
           sigma_ref, star_ref, *scratch):
    r = SimpleNamespace(**dict(zip(names, scratch)))
    g, x, zh, y = position()
    me = x * 8 + zh * 4 + y
    mine = zh * 4 + g
    step, mode0 = zh, g * 3

    def first(s):
        return (x * 8 + y) * 128 + lax.rem(s, 4) * 4096 + s // 4 * 512

    loads = [pltpu.make_async_copy(src, dst, r.in_sem.at[i]) for i, (src, dst) in enumerate(
        ((u_ref, r.uin), (en_ref, r.en), (mask_ref, r.mask), (lat_ref, r.lat), (kq_ref, r.kq), (irr_ref, r.irr)))]
    for copy in loads:
        copy.start()

    barrier = pltpu.get_barrier_semaphore()
    friends = [at(g2, x, zh2, y) for _, g2, zh2 in column(g, zh)] + [(g, (me + hop) % 32) for hop in range(1, 32)]
    for device in friends:
        pl.semaphore_signal(barrier, inc=1, device_id=device, device_id_type=MESH)

    def part(at_step, triple, c, m):
        return g_ref.at[at_step, :, pl.ds(pl.multiple_of(c * 3072 + triple * 768 + m * 256, 256), 256)]

    near = []
    for c in range(2):
        for m in range(3):
            near.append(pltpu.make_async_copy(part(zh, g, c, m), r.g.at[m, c, x, zh, y], r.near_sem.at[c, m]))
            near[-1].start()
    pl.semaphore_wait(barrier, len(friends))

    pz, pg = 1 - zh, (g + 2) % 4
    far = []
    for c in range(2):
        for m in range(3):
            far.append(remote(part(pz, pg, c, m), r.g.at[m, c, x, zh, y], r.z_send.at[c, m], r.z_recv.at[c, m],
                              at(pg, x, pz, y)))
            far[-1].start()
    sent = list(far)

    def go(copy):
        copy.start()
        sent.append(copy)

    def plane(hop, along_x):
        return at(g, (x + hop) % 4, zh, y) if along_x else at(g, x, zh, (y + hop) % 4)

    def first_leg(c, half, z):
        piece = r.g.at[:, c, x, z, y]
        for hop in (1, 3, 2):
            go(remote(piece, piece, r.p_send.at[c, half, hop], r.p_recv.at[c, half, hop], plane(hop, c == 0)))

    for copy in near:
        copy.wait()
    for c in range(2):
        first_leg(c, 0, zh)

    loads[0].wait()
    r.u[mine] = r.uin[...].astype(BF16)
    loads[1].wait()
    loads[2].wait()
    r.e[mine, 0:16] = r.en[...]
    r.e[mine, 16:32] = r.mask[...].astype(F32)
    small = []
    for hop, g2, zh2 in column(g, zh):
        device = at(g2, x, zh2, y)
        small.append(remote(r.u.at[mine], r.u.at[mine], r.u_send.at[hop], r.u_recv.at[hop], device))
        small.append(remote(r.e.at[mine], r.e.at[mine], r.e_send.at[hop], r.e_recv.at[hop], device))
        small[-2].start()
        small[-1].start()

    constants(r)
    loads[4].wait()
    partner_order(r, r.kq[...], step)
    loads[3].wait()
    tables(r, r.lat[...], first)
    for copy in far:
        copy.wait_recv()
    for c in range(2):
        first_leg(c, 1, 1 - zh)

    def second_leg(m, c, hop):
        xs, ys = ((x + 4 - hop) % 4, y) if c == 0 else (x, (y + 4 - hop) % 4)
        piece = r.g.at[m, c, xs, :, ys]
        for to in (1, 3, 2):
            go(remote(piece, piece, r.g_send.at[c, m, 4 * hop + to], r.g_recv.at[c, m, 4 * hop + to],
                      plane(to, c == 1)))

    for m in range(3):
        for hop in (0, 1, 3, 2):
            for c in range(2):
                if m == 0 and hop:
                    for half in range(2):
                        z = zh if half == 0 else 1 - zh
                        xs, ys = ((x + 4 - hop) % 4, y) if c == 0 else (x, (y + 4 - hop) % 4)
                        piece = r.g.at[:, c, xs, z, ys]
                        remote(piece, piece, r.p_send.at[c, half, hop], r.p_recv.at[c, half, hop],
                               plane(hop, c == 0)).wait_recv()
                second_leg(m, c, hop)

    loop(lambda s: phases(r, s, first))
    for copy in small:
        copy.wait_recv()
    sent += small
    loop(lambda s: levels(r, s, step))
    loop(lambda s: rotations(r, s, step))
    onsite, phonon, bose = mode_terms(freq, froh, step, mode0)

    def arrived(m):
        for hop in (0, 1, 3, 2):
            for to in (1, 3, 2):
                for c in range(2):
                    a, b = (hop, to) if c == 0 else (to, hop)
                    piece = r.g.at[m, c, (x + 4 - a) % 4, :, (y + 4 - b) % 4]
                    remote(piece, piece, r.g_send.at[c, m, 4 * hop + to], r.g_recv.at[c, m, 4 * hop + to],
                           plane(to, c == 1)).wait_recv()

    for m in range(3):
        arrived(m)
        vertex(r, m, 0, onsite[m])
        if m:
            regroup_vertex(r, m - 1, 1)
        vertex(r, m, 1, onsite[m])
        regroup_vertex(r, m, 0)
    regroup_vertex(r, 2, 1)
    loop(lambda s: self_energy(r, s, bose, phonon))
    total = band_sum(r)
    for s in range(8):
        r.part[s] = total[s * 32:s * 32 + 32]

    sums = []
    for hop, g2, zh2 in column(g, zh):
        sums.append(remote(r.part.at[zh2 * 4 + g2], r.got.at[hop], r.a_send.at[hop], r.a_recv.at[hop],
                           at(g2, x, zh2, y)))
        go(sums[-1])
    loads[5].wait()
    member = jnp.where(iota((512, 128), 0) == r.irr[...], 1.0, 0.0).astype(BF16)
    total = r.part[mine]
    for hop, copy in enumerate(sums, 1):
        copy.wait_recv()
        total = total + r.got[hop]
    sigma_ref[0] = total[0:16]
    sigma_ref[1] = total[16:32]
    columns = jnp.concatenate(pieces(total, 3) + [jnp.ones((32, 128), BF16)], 0)
    r.stars[...] = dot_nt(member, columns)
    blocks = []
    for hop in range(1, 32):
        owner = (me + hop) % 32
        blocks.append(remote(r.stars.at[pl.ds(pl.multiple_of(owner * 16, 16), 16)], r.blocks.at[hop],
                             r.b_send.at[hop], r.b_recv.at[hop], (g, owner)))
        go(blocks[-1])
    mean = r.stars[pl.ds(pl.multiple_of(me * 16, 16), 16)]
    for hop, copy in enumerate(blocks, 1):
        copy.wait_recv()
        mean = mean + r.blocks[hop]
    count = pltpu.roll(mean, 32, 1)
    mean = mean + pltpu.roll(mean, 96, 1) + pltpu.roll(mean, 64, 1)
    mean = (mean / jnp.maximum(count, 1.0)).T
    star_ref[0] = mean[0:16]
    star_ref[1] = mean[16:32]
    for copy in sent:
        copy.wait_send()


def local(g_real, lattice, u_rot, energy, band_mask, freq, froh, kq_index, irr_id):
    anywhere = pl.BlockSpec(memory_space=pl.ANY)
    scalars = pl.BlockSpec(memory_space=pltpu.SMEM)
    vm = pl.BlockSpec(memory_space=pltpu.VMEM)
    scratch = {**scratch_shapes(), **io_shapes(), **semaphores()}
    return pl.pallas_call(
        functools.partial(kernel, list(scratch)),
        out_shape=(jax.ShapeDtypeStruct((2, 16, 128), F32), jax.ShapeDtypeStruct((2, 16, 16), F32)),
        in_specs=[anywhere] * 7 + [scalars] * 2,
        out_specs=(vm, vm),
        scratch_shapes=list(scratch.values()),
        compiler_params=pltpu.CompilerParams(collective_id=0, has_side_effects=True,
                                             vmem_limit_bytes=60 * 2 ** 20),
    )(g_real, u_rot.reshape(512, 128), energy, band_mask, lattice, kq_index, irr_id.reshape(1, 128), freq, froh)


def solution(mesh):
    in_specs = (
        P(None, "kp", None),
        P(),
        P(None, None, None, ("grp", "kp")),
        P(None, ("grp", "kp")),
        P(None, ("grp", "kp")),
        P(),
        P(),
        P(),
        P(("grp", "kp")),
    )
    out_specs = (P(None, None, ("grp", "kp")), P(None, None, ("grp", "kp")))
    return jax.shard_map(local, mesh=mesh, in_specs=in_specs, out_specs=out_specs, check_vma=False)
```

```python
import functools
import math
from types import SimpleNamespace

import jax
import jax.numpy as jnp
from jax import lax
from jax.experimental import pallas as pl
from jax.experimental.pallas import tpu as pltpu
from jax.sharding import PartitionSpec as P

KT = 0.025
ETA = 0.05
NKM = 40
F32, BF16 = jnp.float32, jnp.bfloat16
NT = (((1,), (1,)), ((), ()))
MESH = pl.DeviceIdType.MESH


def mod_mesh(values):
    return values - NKM * jnp.floor((values + 0.5) * (1.0 / NKM))


def turn(steps):
    x = (steps - 20.0) * (1.0 / 20.0)
    y = x * x
    cos, sin = 0.0, 0.0
    for n in range(8, -1, -1):
        cos = cos * y + (-1.0) ** n * math.pi ** (2 * n) / math.factorial(2 * n)
        sin = sin * y + (-1.0) ** n * math.pi ** (2 * n + 1) / math.factorial(2 * n + 1)
    return -cos, -(sin * x)


def pieces(x, count):
    out = []
    for _ in range(count):
        head = x.astype(BF16)
        out.append(head)
        x = x - head.astype(F32)
    return out


def dot(a, b):
    return jnp.dot(a, b, preferred_element_type=F32)


def dot_nt(a, b):
    return lax.dot_general(a, b, NT, preferred_element_type=F32)


def iota(shape, axis):
    return lax.broadcasted_iota(jnp.int32, shape, axis)


def together(work):
    while work:
        work = [w for w in work if next(w, work) is not work]


def swap_groups(parts):
    parts = list(parts)
    lane = iota(parts[0].shape, 1)
    for bit in (1, 2, 4):
        mask = (lane & (16 * bit)) != 0
        for low in range(8):
            if low & bit == 0:
                a, b = parts[low], parts[low | bit]
                parts[low] = jnp.where(mask, pltpu.roll(b, 16 * bit, 1), a)
                parts[low | bit] = jnp.where(mask, b, pltpu.roll(a, 128 - 16 * bit, 1))
    return parts


def scratch_shapes():
    vm = pltpu.VMEM
    return dict(
        g=vm((3, 2, 4, 2, 4, 32, 256), BF16),
        u=vm((8, 512, 128), BF16),
        e=vm((8, 32, 128), F32),
        ac=vm((40, 1024), F32), as_=vm((40, 1024), F32),
        bc=vm((128, 1024), F32), bs=vm((128, 1024), F32),
        ph=vm((8, 256, 2048), BF16),
        v=vm((2, 1024, 256), BF16),
        xs=vm((2, 8, 2, 256, 128), BF16),
        t1=vm((8, 3, 256, 256), BF16),
        t2=vm((2, 6, 128, 256), BF16),
        t3=vm((2, 6, 256, 128), BF16),
        ex=vm((128, 2048), F32), fa=vm((64, 2048), F32),
        sums=vm((256, 2048), F32),
        rep=vm((128, 2048), BF16), rept=vm((2048, 128), BF16), diag=vm((128, 128), BF16), eye=vm((128, 128), BF16),
        mix=vm((256, 256), BF16), perm=vm((128, 128), BF16), turned=vm((128, 128), BF16),
    )


def constants(r):
    rr, rl = iota((128, 2048), 0), iota((128, 2048), 1)
    r.rep[...] = jnp.where(rl // 16 == rr, 1.0, 0.0).astype(BF16)
    rr, rl = iota((2048, 128), 0), iota((2048, 128), 1)
    r.rept[...] = jnp.where(rr // 16 == rl, 1.0, 0.0).astype(BF16)
    sr, sl = iota((128, 128), 0), iota((128, 128), 1)
    r.diag[...] = jnp.where(sr // 16 == sl // 16, 1.0, 0.0).astype(BF16)
    br, bl = iota((256, 256), 0), iota((256, 256), 1)
    r.eye[...] = jnp.where(sr == sl, 1.0, 0.0).astype(BF16)
    r.mix[...] = jnp.where((br // 16 == bl % 16) & (br % 16 == bl // 16), 1.0, 0.0).astype(BF16)


def partner_order(r, kq, step):
    sr, sl = iota((128, 128), 0), iota((128, 128), 1)
    order = jnp.where(step == 0, kq[0:1, :], kq[1:2, :])
    perm = jnp.where(sr == order, 1.0, 0.0).T.astype(BF16)
    r.perm[...] = perm
    regroup = jnp.where((sr // 16 == sl % 8) & (sr % 16 == sl // 8), 1.0, 0.0).astype(BF16)
    r.turned[...] = dot(regroup, perm).astype(BF16)


def tables(r, lattice, first):
    lat = lattice.astype(F32)
    r.ac[...], r.as_[...] = turn(mod_mesh(iota((40, 1024), 0).astype(F32) * lat[0:1]))
    row16 = iota((16, 1024), 0).astype(F32)

    def one(s, carry):
        i0 = row16 * 8.0 + first(s).astype(F32) + 0.5
        n2 = mod_mesh(jnp.floor(i0 * (1.0 / 40.0)))
        n3 = mod_mesh(jnp.floor(i0 * (1.0 / 1600.0)))
        rows = pl.ds(pl.multiple_of(s * 16, 16), 16)
        r.bc[rows], r.bs[rows] = turn(mod_mesh(n2 * lat[1:2] + n3 * lat[2:3]))
        return carry

    lax.fori_loop(0, 8, one, 0)


def phases(r, s, first):
    base = first(s)

    def pair(o2, carry):
        cs, sn = [], []
        for h in range(2):
            o = o2 * 2 + h
            rows = pl.ds(pl.multiple_of(lax.rem(base + o * 8, NKM), 8), 8)
            a_c, a_s = r.ac[rows], r.as_[rows]
            b_c, b_s = r.bc[pl.ds(s * 16 + o, 1)], r.bs[pl.ds(s * 16 + o, 1)]
            cs.append(a_c * b_c - a_s * b_s)
            sn.append(a_s * b_c + a_c * b_s)
        co = jnp.concatenate(cs, 0).astype(BF16)
        si = jnp.concatenate(sn, 0)
        up = pl.ds(pl.multiple_of(o2 * 16, 16), 16)
        low = pl.ds(pl.multiple_of(o2 * 16 + 128, 16), 16)
        r.ph[s, up, 0:1024] = co
        r.ph[s, up, 1024:2048] = (-si).astype(BF16)
        r.ph[s, low, 0:1024] = si.astype(BF16)
        r.ph[s, low, 1024:2048] = co
        return carry

    lax.fori_loop(0, 8, pair, 0)


def partner_set(s, step):
    return s // 4 * 4 + lax.rem(lax.rem(s, 4) + step + 1, 4)


def levels(r, s, step):
    own = pieces(r.e[s, 0:16], 3)
    far = partner_set(s, step)
    far_e = pieces(r.e[far, 0:16], 3) + [r.e[far, 16:32].astype(BF16)]
    moved = dot_nt(jnp.concatenate(far_e, 0), r.perm[...]).astype(BF16)
    yield
    both = dot(jnp.concatenate(own + [moved], 0), r.rep[...])
    yield
    r.ex[pl.ds(pl.multiple_of(s * 16, 16), 16)] = both[0:16] + both[16:32] + both[32:48]
    pick = iota((16, 2048), 0) == iota((16, 2048), 1) % 16
    fe = jnp.where(pick, both[48:64] + both[64:80] + both[80:96], 0.0).sum(0, keepdims=True)
    fm = jnp.where(pick, both[96:112], 0.0).sum(0, keepdims=True)
    occ = 1.0 / (jnp.exp(fe * (1.0 / KT)) + 1.0)
    r.fa[pl.ds(pl.multiple_of(s * 8, 8), 8)] = jnp.concatenate([fe, fm, occ, jnp.zeros((5, 2048), F32)], 0)


def regroup_columns(tiles):
    cols = []
    for c in range(2):
        rows = []
        for hi in range(2):
            t = tiles[c][hi]
            rows += swap_groups([t[k * 16:k * 16 + 16] for k in range(8)])
        cols.append(jnp.concatenate(rows, 0))
    return jnp.concatenate(cols, 1)


def regroup_rows(r, tiles):
    return dot(r.mix[...], regroup_columns(tiles)).astype(BF16)


def rotations(r, w, s, step):
    left, at = (r.eye[...], s) if w == 0 else (r.turned[...], partner_set(s, step))
    points = dot_nt(left, r.u[at]).astype(BF16)
    yield
    cols = regroup_columns([[points[:, c * 256 + hi * 128:c * 256 + hi * 128 + 128] for hi in range(2)]
                            for c in range(2)])
    yield
    out = dot(r.mix[...], cols).astype(BF16)
    r.xs[w, s, 0] = out[:, 0:128]
    r.xs[w, s, 1] = out[:, 128:256]


def vertex(r, m, half, onsite):
    rows = r.ph[half * 4:half * 4 + 4].reshape(1024, 2048)
    v = dot(rows, r.g[m].reshape(2048, 256))
    for s in range(4):
        for c in range(2):
            at = s * 256 + c * 128
            r.v[half, at:at + 128] = (v[at:at + 128] + onsite[c]).astype(BF16)


def regroup_vertex(r, m, half):
    for s in range(4):
        parts = [[r.v[half, s * 256 + c * 128:s * 256 + c * 128 + 128, hi * 128:hi * 128 + 128] for hi in range(2)]
                 for c in range(2)]
        r.t1[half * 4 + s, m] = regroup_rows(r, parts)


def block_matrix(r, w, s, o):
    rows = slice(o * 16, o * 16 + 16)
    d = r.diag[...]
    return jnp.concatenate([jnp.concatenate([r.xs[w, s, i, rows]] * 8, 0) * d for i in range(2)], 1)


def self_energy(r, s, lane, bose, phonon):
    for o in range(16):
        rows = slice(o * 16, o * 16 + 16)
        left = jnp.concatenate([r.t1[s, m, rows, c * 128:c * 128 + 128] for c in range(2) for m in range(3)], 0)
        both = dot(left, block_matrix(r, 0, s, o))
        re = (both[0:48, 0:128] - both[48:96, 128:256]).astype(BF16)
        im = (both[0:48, 128:256] + both[48:96, 0:128]).astype(BF16)
        inner = slice(o % 8 * 16, o % 8 * 16 + 16)
        for m in range(3):
            r.t2[lane, o // 8 * 3 + m, inner, 0:128] = re[m * 16:m * 16 + 16]
            r.t2[lane, o // 8 * 3 + m, inner, 128:256] = im[m * 16:m * 16 + 16]
    yield
    for i in range(6):
        r.t3[lane, i] = r.t2[lane, i].T
    yield
    for o in range(16):
        hi, lo = o // 2, o % 2
        left = jnp.concatenate([r.t3[lane, lo * 3 + m, c * 128 + hi * 16:c * 128 + hi * 16 + 16]
                                for c in range(2) for m in range(3)], 0)
        both = dot(left, block_matrix(r, 1, s, o))
        br = both[0:48, 0:128] + both[48:96, 128:256]
        bi = both[48:96, 0:128] - both[0:48, 128:256]
        strength = br * br + bi * bi
        cols = slice(o * 128, o * 128 + 128)
        eo = r.ex[pl.ds(pl.multiple_of(s * 16, 16), 16), cols]
        far = r.fa[pl.ds(pl.multiple_of(s * 8, 8), 8), cols]
        fe, fm, occ = far[0:1], far[1:2], far[2:3]
        diff = eo - fe
        re, im = 0.0, 0.0
        for m in range(3):
            em = fm * (bose[m] + occ)
            ab = fm * (bose[m] + 1.0 - occ)
            up = diff + phonon[m]
            lw = diff - phonon[m]
            du = up * up + ETA * ETA
            dl = lw * lw + ETA * ETA
            scale = strength[m * 16:m * 16 + 16] / (du * dl)
            e1 = em * dl
            a1 = ab * du
            re = re + scale * (e1 * up + a1 * lw)
            im = im + scale * (e1 + a1)
        r.sums[pl.ds(pl.multiple_of(s * 32, 32), 16), cols] = re
        r.sums[pl.ds(pl.multiple_of(s * 32 + 16, 16), 16), cols] = im * (-ETA)


def band_sum(r):
    hi, lo = pieces(r.sums[...], 2)
    return (dot(hi, r.rept[...]) + dot(lo, r.rept[...])) * (1.0 / 384.0)


def mode_terms(freq, froh, step, mode0):
    lane = iota((1, 256), 1)
    site = jnp.where(lane // 16 == lane % 16, 1.0, 0.0)

    def pick(rows, m):
        row = jnp.where(step == 0, rows[0:1], rows[1:2])
        return jnp.where(iota((1, 12), 1) == mode0 + m, row, 0.0).sum(1, keepdims=True)

    onsite = [[site * pick(froh[:, c], m) for c in range(2)] for m in range(3)]
    phonon = [jnp.broadcast_to(pick(freq, m), (1, 128)) for m in range(3)]
    bose = [1.0 / (jnp.exp(w * (1.0 / KT)) - 1.0) for w in phonon]
    return onsite, phonon, bose


def loop(body, count=8):
    def step(s, carry):
        body(s)
        return carry
    lax.fori_loop(0, count, step, 0)


def position():
    kp = lax.axis_index("kp")
    return lax.axis_index("grp"), kp // 8, kp // 4 % 2, kp % 4


def at(g, x, zh, y):
    return (g, x * 8 + zh * 4 + y)


def column(g, zh):
    for hop in range(1, 8):
        other = (zh * 4 + g + hop) % 8
        yield hop, other % 4, other // 4


def remote(src, dst, send, recv, device):
    return pltpu.make_async_remote_copy(src_ref=src, dst_ref=dst, send_sem=send, recv_sem=recv,
                                        device_id=device, device_id_type=MESH)


def semaphores():
    dma = pltpu.SemaphoreType.DMA
    return dict(
        in_sem=dma((8,)), near_sem=dma((2, 3)),
        z_send=dma((2, 3)), z_recv=dma((2, 3)),
        u_send=dma((8,)), u_recv=dma((8,)), e_send=dma((8,)), e_recv=dma((8,)),
        p_send=dma((2, 2, 4)), p_recv=dma((2, 2, 4)),
        g_send=dma((2, 3, 16)), g_recv=dma((2, 3, 16)),
        a_send=dma((8,)), a_recv=dma((8,)), b_send=dma((17,)), b_recv=dma((17,)),
    )


def io_shapes():
    vm = pltpu.VMEM
    return dict(
        uin=vm((512, 128), F32), en=vm((16, 128), F32), mask=vm((16, 128), jnp.int32),
        lat=vm((3, 1024), jnp.int32), kq=vm((2, 128), jnp.int32), irr=vm((1, 128), jnp.int32),
        part=vm((8, 32, 128), F32), got=vm((8, 32, 128), F32),
        stars=vm((4, 2, 4, 16, 128), F32), blocks=vm((16, 2, 16, 128), F32),
        pairs=vm((2, 16, 128), F32), other=vm((16, 128), F32),
        freq=vm((2, 12), F32), froh=vm((2, 2, 12), F32),
    )


def kernel(names, g_ref, u_ref, en_ref, mask_ref, lat_ref, kq_ref, irr_ref, freq_ref, froh_ref,
           sigma_ref, star_ref, *scratch):
    r = SimpleNamespace(**dict(zip(names, scratch)))
    g, x, zh, y = position()
    mine = zh * 4 + g
    step, mode0 = zh, g * 3

    def first(s):
        return (x * 8 + y) * 128 + lax.rem(s, 4) * 4096 + s // 4 * 512

    loads = [pltpu.make_async_copy(src, dst, r.in_sem.at[i]) for i, (src, dst) in enumerate(
        ((u_ref, r.uin), (en_ref, r.en), (mask_ref, r.mask), (lat_ref, r.lat), (kq_ref, r.kq), (irr_ref, r.irr),
         (freq_ref, r.freq), (froh_ref, r.froh)))]
    for copy in loads:
        copy.start()

    barrier = pltpu.get_barrier_semaphore()
    friends = [at(g2, x, zh2, y) for _, g2, zh2 in column(g, zh)] + [
        at(g, (x + i // 4) % 4, zh, (y + i % 4) % 4) for i in range(1, 16)]
    for device in friends:
        pl.semaphore_signal(barrier, inc=1, device_id=device, device_id_type=MESH)

    def part(at_step, triple, c, m):
        return g_ref.at[at_step, :, pl.ds(pl.multiple_of(c * 3072 + triple * 768 + m * 256, 256), 256)]

    near = []
    for c in range(2):
        for m in range(3):
            near.append(pltpu.make_async_copy(part(zh, g, c, m), r.g.at[m, c, x, zh, y], r.near_sem.at[c, m]))
            near[-1].start()
    pl.semaphore_wait(barrier, len(friends))

    pz, pg = 1 - zh, (g + 2) % 4
    far = []
    for c in range(2):
        for m in range(3):
            far.append(remote(part(pz, pg, c, m), r.g.at[m, c, x, zh, y], r.z_send.at[c, m], r.z_recv.at[c, m],
                              at(pg, x, pz, y)))
            far[-1].start()
    sent = list(far)

    def go(copy):
        copy.start()
        sent.append(copy)

    def plane(hop, along_x):
        return at(g, (x + hop) % 4, zh, y) if along_x else at(g, x, zh, (y + hop) % 4)

    def first_leg(c, half, z):
        piece = r.g.at[:, c, x, z, y]
        for hop in (1, 3, 2):
            go(remote(piece, piece, r.p_send.at[c, half, hop], r.p_recv.at[c, half, hop], plane(hop, c == 0)))

    chip, sibling = mine // 2, at(g // 2 * 2 + 1 - g % 2, x, zh, y)

    def share(slot, sem, device):
        for buf, send, recv in ((r.u, r.u_send, r.u_recv), (r.e, r.e_send, r.e_recv)):
            go(remote(buf.at[slot], buf.at[slot], send.at[sem], recv.at[sem], device))

    def shared(slot, sem):
        for buf, send, recv in ((r.u, r.u_send, r.u_recv), (r.e, r.e_send, r.e_recv)):
            remote(buf.at[slot], buf.at[slot], send.at[sem], recv.at[sem], sibling).wait_recv()

    for i in range(3):
        loads[i].wait()
    r.u[mine] = r.uin[...].astype(BF16)
    r.e[mine, 0:16] = r.en[...]
    r.e[mine, 16:32] = r.mask[...].astype(F32)
    for hop in (1, 3, 2):
        there = (chip + hop) % 4
        share(mine, hop, at(there % 2 * 2 + g % 2, x, there // 2, y))
    share(mine, 0, sibling)

    for copy in near:
        copy.wait()
    for c in range(2):
        first_leg(c, 0, zh)
    constants(r)
    loads[4].wait()
    partner_order(r, r.kq[...], step)
    loads[3].wait()
    tables(r, r.lat[...], first)
    for copy in far:
        copy.wait_recv()
    for c in range(2):
        first_leg(c, 1, 1 - zh)
    loop(lambda s: phases(r, s, first))

    def second_leg(m, c, hop):
        xs, ys = ((x + 4 - hop) % 4, y) if c == 0 else (x, (y + 4 - hop) % 4)
        piece = r.g.at[m, c, xs, :, ys]
        for to in (1, 3, 2):
            go(remote(piece, piece, r.g_send.at[c, m, 4 * hop + to], r.g_recv.at[c, m, 4 * hop + to],
                      plane(to, c == 1)))

    for m in range(3):
        for hop in (0, 1, 3, 2):
            for c in range(2):
                if m == 0 and hop:
                    for half in range(2):
                        z = zh if half == 0 else 1 - zh
                        xs, ys = ((x + 4 - hop) % 4, y) if c == 0 else (x, (y + 4 - hop) % 4)
                        piece = r.g.at[:, c, xs, z, ys]
                        remote(piece, piece, r.p_send.at[c, half, hop], r.p_recv.at[c, half, hop],
                               plane(hop, c == 0)).wait_recv()
                second_leg(m, c, hop)

    for hop in (1, 3, 2):
        shared((chip + 4 - hop) % 4 * 2 + g % 2, hop)
        share((chip + 4 - hop) % 4 * 2 + g % 2, 4 + hop, sibling)
    shared(chip * 2 + 1 - g % 2, 0)
    for hop in (1, 3, 2):
        shared((chip + 4 - hop) % 4 * 2 + 1 - g % 2, 4 + hop)
    loop(lambda i: together([levels(r, i * 4 + q, step) for q in range(4)]), 2)
    loop(lambda i: together([rotations(r, w, i * 4 + q, step) for q in range(4) for w in range(2)]), 2)
    loads[6].wait()
    loads[7].wait()
    onsite, phonon, bose = mode_terms(r.freq[...], r.froh[...], step, mode0)

    def arrived(m):
        for hop in (0, 1, 3, 2):
            for to in (1, 3, 2):
                for c in range(2):
                    a, b = (hop, to) if c == 0 else (to, hop)
                    piece = r.g.at[m, c, (x + 4 - a) % 4, :, (y + 4 - b) % 4]
                    remote(piece, piece, r.g_send.at[c, m, 4 * hop + to], r.g_recv.at[c, m, 4 * hop + to],
                           plane(to, c == 1)).wait_recv()

    for m in range(3):
        arrived(m)
        vertex(r, m, 0, onsite[m])
        if m:
            regroup_vertex(r, m - 1, 1)
        vertex(r, m, 1, onsite[m])
        regroup_vertex(r, m, 0)
    regroup_vertex(r, 2, 1)
    loop(lambda i: together([self_energy(r, 2 * i + q, q, bose, phonon) for q in range(2)]), 4)
    total = band_sum(r)
    for s in range(8):
        r.part[s] = total[s * 32:s * 32 + 32]

    sums = []
    for hop, g2, zh2 in column(g, zh):
        sums.append(remote(r.part.at[zh2 * 4 + g2], r.got.at[hop], r.a_send.at[hop], r.a_recv.at[hop],
                           at(g2, x, zh2, y)))
        go(sums[-1])
    loads[5].wait()
    member = jnp.where(iota((512, 128), 0) == r.irr[...], 1.0, 0.0).astype(BF16)
    total = r.part[mine]
    for hop, copy in enumerate(sums, 1):
        copy.wait_recv()
        total = total + r.got[hop]
    sigma_ref[0] = total[0:16]
    sigma_ref[1] = total[16:32]
    columns = jnp.concatenate(pieces(total, 3) + [jnp.ones((32, 128), BF16)], 0)
    r.stars[...] = dot_nt(member, columns).reshape(4, 2, 4, 16, 128)
    blocks = []
    for i in range(1, 16):
        xs, ys = (x + i // 4) % 4, (y + i % 4) % 4
        blocks.append(remote(r.stars.at[xs, :, ys], r.blocks.at[i], r.b_send.at[i], r.b_recv.at[i],
                             at(g, xs, zh, ys)))
        go(blocks[-1])
    mean = r.stars[x, :, y]
    for i, copy in enumerate(blocks, 1):
        copy.wait_recv()
        mean = mean + r.blocks[i]
    r.pairs[...] = mean
    last = remote(r.pairs.at[1 - zh], r.other, r.b_send.at[16], r.b_recv.at[16], at(g, x, 1 - zh, y))
    go(last)
    mean = r.pairs[zh]
    last.wait_recv()
    mean = mean + r.other[...]
    count = pltpu.roll(mean, 32, 1)
    mean = mean + pltpu.roll(mean, 96, 1) + pltpu.roll(mean, 64, 1)
    mean = (mean / jnp.maximum(count, 1.0)).T
    star_ref[0] = mean[0:16]
    star_ref[1] = mean[16:32]
    for copy in sent:
        copy.wait_send()


def local(g_real, lattice, u_rot, energy, band_mask, freq, froh, kq_index, irr_id):
    anywhere = pl.BlockSpec(memory_space=pl.ANY)
    vm = pl.BlockSpec(memory_space=pltpu.VMEM)
    scratch = {**scratch_shapes(), **io_shapes(), **semaphores()}
    return pl.pallas_call(
        functools.partial(kernel, list(scratch)),
        out_shape=(jax.ShapeDtypeStruct((2, 16, 128), F32), jax.ShapeDtypeStruct((2, 16, 16), F32)),
        in_specs=[anywhere] * 9,
        out_specs=(vm, vm),
        scratch_shapes=list(scratch.values()),
        compiler_params=pltpu.CompilerParams(collective_id=0, has_side_effects=True,
                                             vmem_limit_bytes=60 * 2 ** 20),
    )(g_real, u_rot.reshape(512, 128), energy, band_mask, lattice, kq_index, irr_id.reshape(1, 128), freq, froh)


def solution(mesh):
    in_specs = (
        P(None, "kp", None),
        P(),
        P(None, None, None, ("grp", "kp")),
        P(None, ("grp", "kp")),
        P(None, ("grp", "kp")),
        P(),
        P(),
        P(),
        P(("grp", "kp")),
    )
    out_specs = (P(None, None, ("grp", "kp")), P(None, None, ("grp", "kp")))
    return jax.shard_map(local, mesh=mesh, in_specs=in_specs, out_specs=out_specs, check_vma=False)
```

```python
import functools
import math
from types import SimpleNamespace

import jax
import jax.numpy as jnp
from jax import lax
from jax.experimental import pallas as pl
from jax.experimental.pallas import tpu as pltpu
from jax.sharding import PartitionSpec as P

KT = 0.025
ETA = 0.05
NKM = 40
F32, BF16 = jnp.float32, jnp.bfloat16
NT = (((1,), (1,)), ((), ()))
MESH = pl.DeviceIdType.MESH


def mod_mesh(values):
    return values - NKM * jnp.floor((values + 0.5) * (1.0 / NKM))


def turn(steps):
    x = (steps - 20.0) * (1.0 / 20.0)
    y = x * x
    cos, sin = 0.0, 0.0
    for n in range(8, -1, -1):
        cos = cos * y + (-1.0) ** n * math.pi ** (2 * n) / math.factorial(2 * n)
        sin = sin * y + (-1.0) ** n * math.pi ** (2 * n + 1) / math.factorial(2 * n + 1)
    return -cos, -(sin * x)


def pieces(x, count):
    out = []
    for _ in range(count):
        head = x.astype(BF16)
        out.append(head)
        x = x - head.astype(F32)
    return out


def dot(a, b):
    return jnp.dot(a, b, preferred_element_type=F32)


def dot_nt(a, b):
    return lax.dot_general(a, b, NT, preferred_element_type=F32)


def iota(shape, axis):
    return lax.broadcasted_iota(jnp.int32, shape, axis)


def together(work):
    while work:
        work = [w for w in work if next(w, work) is not work]


def swap_groups(parts):
    parts = list(parts)
    lane = iota(parts[0].shape, 1)
    for bit in (1, 2, 4):
        mask = (lane & (16 * bit)) != 0
        for low in range(8):
            if low & bit == 0:
                a, b = parts[low], parts[low | bit]
                parts[low] = jnp.where(mask, pltpu.roll(b, 16 * bit, 1), a)
                parts[low | bit] = jnp.where(mask, b, pltpu.roll(a, 128 - 16 * bit, 1))
    return parts


def scratch_shapes():
    vm = pltpu.VMEM
    return dict(
        g=vm((3, 2, 4, 2, 4, 32, 256), BF16),
        u=vm((8, 512, 128), BF16),
        e=vm((8, 32, 128), F32),
        ac=vm((40, 1024), F32), as_=vm((40, 1024), F32),
        bc=vm((128, 1024), F32), bs=vm((128, 1024), F32),
        ph=vm((8, 256, 2048), BF16),
        v=vm((2, 1024, 256), BF16),
        xs=vm((2, 8, 2, 256, 128), BF16),
        t1=vm((8, 3, 256, 256), BF16),
        t2=vm((2, 6, 128, 256), BF16),
        t3=vm((2, 6, 256, 128), BF16),
        ex=vm((128, 2048), F32), fa=vm((64, 2048), F32),
        sums=vm((256, 2048), F32),
        rep=vm((128, 2048), BF16), rept=vm((2048, 128), BF16), diag=vm((128, 128), BF16), eye=vm((128, 128), BF16),
        mix=vm((256, 256), BF16), perm=vm((128, 128), BF16), turned=vm((128, 128), BF16),
    )


def constants(r):
    rr, rl = iota((128, 2048), 0), iota((128, 2048), 1)
    r.rep[...] = jnp.where(rl // 16 == rr, 1.0, 0.0).astype(BF16)
    rr, rl = iota((2048, 128), 0), iota((2048, 128), 1)
    r.rept[...] = jnp.where(rr // 16 == rl, 1.0, 0.0).astype(BF16)
    sr, sl = iota((128, 128), 0), iota((128, 128), 1)
    r.diag[...] = jnp.where(sr // 16 == sl // 16, 1.0, 0.0).astype(BF16)
    br, bl = iota((256, 256), 0), iota((256, 256), 1)
    r.eye[...] = jnp.where(sr == sl, 1.0, 0.0).astype(BF16)
    r.mix[...] = jnp.where((br // 16 == bl % 16) & (br % 16 == bl // 16), 1.0, 0.0).astype(BF16)


def partner_order(r, kq, step):
    sr, sl = iota((128, 128), 0), iota((128, 128), 1)
    order = jnp.where(step == 0, kq[0:1, :], kq[1:2, :])
    perm = jnp.where(sr == order, 1.0, 0.0).T.astype(BF16)
    r.perm[...] = perm
    regroup = jnp.where((sr // 16 == sl % 8) & (sr % 16 == sl // 8), 1.0, 0.0).astype(BF16)
    r.turned[...] = dot(regroup, perm).astype(BF16)


def tables(r, lattice, first):
    lat = lattice.astype(F32)
    r.ac[...], r.as_[...] = turn(mod_mesh(iota((40, 1024), 0).astype(F32) * lat[0:1]))
    row16 = iota((16, 1024), 0).astype(F32)

    def one(s, carry):
        i0 = row16 * 8.0 + first(s).astype(F32) + 0.5
        n2 = mod_mesh(jnp.floor(i0 * (1.0 / 40.0)))
        n3 = mod_mesh(jnp.floor(i0 * (1.0 / 1600.0)))
        rows = pl.ds(pl.multiple_of(s * 16, 16), 16)
        r.bc[rows], r.bs[rows] = turn(mod_mesh(n2 * lat[1:2] + n3 * lat[2:3]))
        return carry

    lax.fori_loop(0, 8, one, 0)


def phases(r, s, first):
    base = first(s)

    def pair(o2, carry):
        cs, sn = [], []
        for h in range(2):
            o = o2 * 2 + h
            rows = pl.ds(pl.multiple_of(lax.rem(base + o * 8, NKM), 8), 8)
            a_c, a_s = r.ac[rows], r.as_[rows]
            b_c, b_s = r.bc[pl.ds(s * 16 + o, 1)], r.bs[pl.ds(s * 16 + o, 1)]
            cs.append(a_c * b_c - a_s * b_s)
            sn.append(a_s * b_c + a_c * b_s)
        co = jnp.concatenate(cs, 0).astype(BF16)
        si = jnp.concatenate(sn, 0)
        up = pl.ds(pl.multiple_of(o2 * 16, 16), 16)
        low = pl.ds(pl.multiple_of(o2 * 16 + 128, 16), 16)
        r.ph[s, up, 0:1024] = co
        r.ph[s, up, 1024:2048] = (-si).astype(BF16)
        r.ph[s, low, 0:1024] = si.astype(BF16)
        r.ph[s, low, 1024:2048] = co
        return carry

    lax.fori_loop(0, 8, pair, 0)


def partner_set(s, step):
    return s // 4 * 4 + lax.rem(lax.rem(s, 4) + step + 1, 4)


def levels(r, s, step):
    own = pieces(r.e[s, 0:16], 3)
    far = partner_set(s, step)
    far_e = pieces(r.e[far, 0:16], 3) + [r.e[far, 16:32].astype(BF16)]
    moved = dot_nt(jnp.concatenate(far_e, 0), r.perm[...]).astype(BF16)
    yield
    both = dot(jnp.concatenate(own + [moved], 0), r.rep[...])
    yield
    r.ex[pl.ds(pl.multiple_of(s * 16, 16), 16)] = both[0:16] + both[16:32] + both[32:48]
    pick = iota((16, 2048), 0) == iota((16, 2048), 1) % 16
    fe = jnp.where(pick, both[48:64] + both[64:80] + both[80:96], 0.0).sum(0, keepdims=True)
    fm = jnp.where(pick, both[96:112], 0.0).sum(0, keepdims=True)
    occ = 1.0 / (jnp.exp(fe * (1.0 / KT)) + 1.0)
    r.fa[pl.ds(pl.multiple_of(s * 8, 8), 8)] = jnp.concatenate([fe, fm, occ, jnp.zeros((5, 2048), F32)], 0)


def regroup_columns(tiles):
    cols = []
    for c in range(2):
        rows = []
        for hi in range(2):
            t = tiles[c][hi]
            rows += swap_groups([t[k * 16:k * 16 + 16] for k in range(8)])
        cols.append(jnp.concatenate(rows, 0))
    return jnp.concatenate(cols, 1)


def regroup_rows(r, tiles):
    return dot(r.mix[...], regroup_columns(tiles)).astype(BF16)


def rotations(r, w, s, step):
    left, at = (r.eye[...], s) if w == 0 else (r.turned[...], partner_set(s, step))
    points = dot_nt(left, r.u[at]).astype(BF16)
    yield
    cols = regroup_columns([[points[:, c * 256 + hi * 128:c * 256 + hi * 128 + 128] for hi in range(2)]
                            for c in range(2)])
    yield
    out = dot(r.mix[...], cols).astype(BF16)
    r.xs[w, s, 0] = out[:, 0:128]
    r.xs[w, s, 1] = out[:, 128:256]


def vertex(r, m, half, onsite):
    rows = r.ph[half * 4:half * 4 + 4].reshape(1024, 2048)
    v = dot(rows, r.g[m].reshape(2048, 256))
    for s in range(4):
        for c in range(2):
            at = s * 256 + c * 128
            r.v[half, at:at + 128] = (v[at:at + 128] + onsite[c]).astype(BF16)


def regroup_vertex(r, m, half):
    for s in range(4):
        parts = [[r.v[half, s * 256 + c * 128:s * 256 + c * 128 + 128, hi * 128:hi * 128 + 128] for hi in range(2)]
                 for c in range(2)]
        r.t1[half * 4 + s, m] = regroup_rows(r, parts)


def block_matrix(r, w, s, o):
    rows = slice(o * 16, o * 16 + 16)
    d = r.diag[...]
    return jnp.concatenate([jnp.concatenate([r.xs[w, s, i, rows]] * 8, 0) * d for i in range(2)], 1)


def self_energy(r, s, lane, bose, phonon):
    for o in range(16):
        rows = slice(o * 16, o * 16 + 16)
        left = jnp.concatenate([r.t1[s, m, rows, c * 128:c * 128 + 128] for c in range(2) for m in range(3)], 0)
        both = dot(left, block_matrix(r, 0, s, o))
        re = (both[0:48, 0:128] - both[48:96, 128:256]).astype(BF16)
        im = (both[0:48, 128:256] + both[48:96, 0:128]).astype(BF16)
        inner = slice(o % 8 * 16, o % 8 * 16 + 16)
        for m in range(3):
            r.t2[lane, o // 8 * 3 + m, inner, 0:128] = re[m * 16:m * 16 + 16]
            r.t2[lane, o // 8 * 3 + m, inner, 128:256] = im[m * 16:m * 16 + 16]
    yield
    for i in range(6):
        r.t3[lane, i] = r.t2[lane, i].T
    yield
    for o in range(16):
        hi, lo = o // 2, o % 2
        left = jnp.concatenate([r.t3[lane, lo * 3 + m, c * 128 + hi * 16:c * 128 + hi * 16 + 16]
                                for c in range(2) for m in range(3)], 0)
        both = dot(left, block_matrix(r, 1, s, o))
        br = both[0:48, 0:128] + both[48:96, 128:256]
        bi = both[48:96, 0:128] - both[0:48, 128:256]
        strength = br * br + bi * bi
        cols = slice(o * 128, o * 128 + 128)
        eo = r.ex[pl.ds(pl.multiple_of(s * 16, 16), 16), cols]
        far = r.fa[pl.ds(pl.multiple_of(s * 8, 8), 8), cols]
        fe, fm, occ = far[0:1], far[1:2], far[2:3]
        diff = eo - fe
        re, im = 0.0, 0.0
        for m in range(3):
            em = fm * (bose[m] + occ)
            ab = fm * (bose[m] + 1.0 - occ)
            up = diff + phonon[m]
            lw = diff - phonon[m]
            du = up * up + ETA * ETA
            dl = lw * lw + ETA * ETA
            scale = strength[m * 16:m * 16 + 16] / (du * dl)
            e1 = em * dl
            a1 = ab * du
            re = re + scale * (e1 * up + a1 * lw)
            im = im + scale * (e1 + a1)
        r.sums[pl.ds(pl.multiple_of(s * 32, 32), 16), cols] = re
        r.sums[pl.ds(pl.multiple_of(s * 32 + 16, 16), 16), cols] = im * (-ETA)


def band_sum(r):
    hi, lo = pieces(r.sums[...], 2)
    return (dot(hi, r.rept[...]) + dot(lo, r.rept[...])) * (1.0 / 384.0)


def mode_terms(freq, froh, step, mode0):
    lane = iota((1, 256), 1)
    site = jnp.where(lane // 16 == lane % 16, 1.0, 0.0)

    def pick(rows, m):
        row = jnp.where(step == 0, rows[0:1], rows[1:2])
        return jnp.where(iota((1, 12), 1) == mode0 + m, row, 0.0).sum(1, keepdims=True)

    onsite = [[site * pick(froh[:, c], m) for c in range(2)] for m in range(3)]
    phonon = [jnp.broadcast_to(pick(freq, m), (1, 128)) for m in range(3)]
    bose = [1.0 / (jnp.exp(w * (1.0 / KT)) - 1.0) for w in phonon]
    return onsite, phonon, bose


def loop(body, count=8):
    def step(s, carry):
        body(s)
        return carry
    lax.fori_loop(0, count, step, 0)


def position():
    kp = lax.axis_index("kp")
    return lax.axis_index("grp"), kp // 8, kp // 4 % 2, kp % 4


def at(g, x, zh, y):
    return (g, x * 8 + zh * 4 + y)


def column(g, zh):
    for hop in range(1, 8):
        other = (zh * 4 + g + hop) % 8
        yield hop, other % 4, other // 4


def remote(src, dst, send, recv, device):
    return pltpu.make_async_remote_copy(src_ref=src, dst_ref=dst, send_sem=send, recv_sem=recv,
                                        device_id=device, device_id_type=MESH)


def semaphores():
    dma = pltpu.SemaphoreType.DMA
    return dict(
        in_sem=dma((8,)), near_sem=dma((1,)), z_sem=dma((2,)), p_sem=dma((2,)), g_send=dma((1,)), g_recv=dma((3,)),
        u_send=dma((1,)), u_recv=dma((4,)), e_send=dma((1,)), e_recv=dma((4,)), a_sem=dma((2,)), b_sem=dma((2,)),
    )


def io_shapes():
    vm = pltpu.VMEM
    return dict(
        uin=vm((512, 128), F32), en=vm((16, 128), F32), mask=vm((16, 128), jnp.int32),
        lat=vm((3, 1024), jnp.int32), kq=vm((2, 128), jnp.int32), irr=vm((1, 128), jnp.int32),
        part=vm((8, 32, 128), F32), got=vm((8, 32, 128), F32),
        stars=vm((512, 128), F32), blocks=vm((32, 16, 128), F32),
        freq=vm((2, 12), F32), froh=vm((2, 2, 12), F32),
    )


def kernel(names, g_ref, u_ref, en_ref, mask_ref, lat_ref, kq_ref, irr_ref, freq_ref, froh_ref,
           sigma_ref, star_ref, *scratch):
    r = SimpleNamespace(**dict(zip(names, scratch)))
    g, x, zh, y = position()
    me = x * 8 + zh * 4 + y
    mine = zh * 4 + g
    step, mode0 = zh, g * 3

    def first(s):
        return (x * 8 + y) * 128 + lax.rem(s, 4) * 4096 + s // 4 * 512

    loads = [pltpu.make_async_copy(src, dst, r.in_sem.at[i]) for i, (src, dst) in enumerate(
        ((u_ref, r.uin), (en_ref, r.en), (mask_ref, r.mask), (lat_ref, r.lat), (kq_ref, r.kq), (irr_ref, r.irr),
         (freq_ref, r.freq), (froh_ref, r.froh)))]
    for copy in loads:
        copy.start()

    barrier = pltpu.get_barrier_semaphore()
    friends = [at(g2, x, zh2, y) for _, g2, zh2 in column(g, zh)] + [(g, (me + hop) % 32) for hop in range(1, 32)]
    for device in friends:
        pl.semaphore_signal(barrier, inc=1, device_id=device, device_id_type=MESH)

    def part(at_step, triple, c, m):
        return g_ref.at[at_step, :, pl.ds(pl.multiple_of(c * 3072 + triple * 768 + m * 256, 256), 256)]

    for c in range(2):
        for m in range(3):
            pltpu.make_async_copy(part(zh, g, c, m), r.g.at[m, c, x, zh, y], r.near_sem.at[0]).start()
    pl.semaphore_wait(barrier, len(friends))

    pz, pg = 1 - zh, (g + 2) % 4
    for c in range(2):
        for m in range(3):
            remote(part(pz, pg, c, m), r.g.at[m, c, x, zh, y], r.z_sem.at[0], r.z_sem.at[1], at(pg, x, pz, y)).start()

    def total(ref, sem):
        pltpu.make_async_copy(ref, ref, sem).wait()

    def plane(hop, along_x):
        return at(g, (x + hop) % 4, zh, y) if along_x else at(g, x, zh, (y + hop) % 4)

    def first_leg(c, z):
        piece = r.g.at[:, c, x, z, y]
        for hop in (1, 3, 2):
            remote(piece, piece, r.p_sem.at[0], r.p_sem.at[1], plane(hop, c == 0)).start()

    chip, sibling = mine // 2, at(g // 2 * 2 + 1 - g % 2, x, zh, y)

    def share(slot, sem, device):
        for buf, send, recv in ((r.u, r.u_send, r.u_recv), (r.e, r.e_send, r.e_recv)):
            remote(buf.at[slot], buf.at[slot], send.at[0], recv.at[sem], device).start()

    def shared(slot, sem):
        for buf, send, recv in ((r.u, r.u_send, r.u_recv), (r.e, r.e_send, r.e_recv)):
            total(buf.at[slot], recv.at[sem])

    for i in range(3):
        loads[i].wait()
    r.u[mine] = r.uin[...].astype(BF16)
    r.e[mine, 0:16] = r.en[...]
    r.e[mine, 16:32] = r.mask[...].astype(F32)
    for hop in (1, 3, 2):
        there = (chip + hop) % 4
        share(mine, hop, at(there % 2 * 2 + g % 2, x, there // 2, y))
    share(mine, 0, sibling)

    total(r.g.at[:, :, x, zh, y], r.near_sem.at[0])
    for c in range(2):
        first_leg(c, zh)
    constants(r)
    loads[4].wait()
    partner_order(r, r.kq[...], step)
    loads[3].wait()
    tables(r, r.lat[...], first)
    total(r.g.at[:, :, x, pz, y], r.z_sem.at[1])
    for c in range(2):
        first_leg(c, 1 - zh)
    loop(lambda s: phases(r, s, first))

    def second_leg(m, c, hop):
        xs, ys = ((x + 4 - hop) % 4, y) if c == 0 else (x, (y + 4 - hop) % 4)
        piece = r.g.at[m, c, xs, :, ys]
        for to in (1, 3, 2):
            remote(piece, piece, r.g_send.at[0], r.g_recv.at[m], plane(to, c == 1)).start()

    for m in range(3):
        for hop in (0, 1, 3, 2):
            for c in range(2):
                if m == 0 and hop == 1 and c == 0:
                    total(r.g.at[:, :, 0:3, :, 0], r.p_sem.at[1])
                second_leg(m, c, hop)

    for hop in (1, 3, 2):
        shared((chip + 4 - hop) % 4 * 2 + g % 2, hop)
        share((chip + 4 - hop) % 4 * 2 + g % 2, 0, sibling)
    total(r.u.at[0:4], r.u_recv.at[0])
    total(r.e.at[0:4], r.e_recv.at[0])
    loop(lambda i: together([levels(r, i * 4 + q, step) for q in range(4)]), 2)
    loop(lambda i: together([rotations(r, w, i * 4 + q, step) for q in range(4) for w in range(2)]), 2)
    loads[6].wait()
    loads[7].wait()
    onsite, phonon, bose = mode_terms(r.freq[...], r.froh[...], step, mode0)

    for m in range(3):
        total(r.g.at[m, :, :, :, 0:3], r.g_recv.at[m])
        vertex(r, m, 0, onsite[m])
        if m:
            regroup_vertex(r, m - 1, 1)
        vertex(r, m, 1, onsite[m])
        regroup_vertex(r, m, 0)
    regroup_vertex(r, 2, 1)
    loop(lambda i: together([self_energy(r, 2 * i + q, q, bose, phonon) for q in range(2)]), 4)
    sums = band_sum(r)
    for s in range(8):
        r.part[s] = sums[s * 32:s * 32 + 32]

    for hop, g2, zh2 in column(g, zh):
        remote(r.part.at[zh2 * 4 + g2], r.got.at[hop], r.a_sem.at[0], r.a_sem.at[1], at(g2, x, zh2, y)).start()
    loads[5].wait()
    member = jnp.where(iota((512, 128), 0) == r.irr[...], 1.0, 0.0).astype(BF16)
    total(r.got.at[1:8], r.a_sem.at[1])
    sigma = r.part[mine]
    for hop in range(1, 8):
        sigma = sigma + r.got[hop]
    sigma_ref[0] = sigma[0:16]
    sigma_ref[1] = sigma[16:32]
    columns = jnp.concatenate(pieces(sigma, 3) + [jnp.ones((32, 128), BF16)], 0)
    r.stars[...] = dot_nt(member, columns)
    for hop in range(1, 32):
        owner = (me + hop) % 32
        remote(r.stars.at[pl.ds(pl.multiple_of(owner * 16, 16), 16)], r.blocks.at[hop],
               r.b_sem.at[0], r.b_sem.at[1], (g, owner)).start()
    mean = r.stars[pl.ds(pl.multiple_of(me * 16, 16), 16)]
    total(r.blocks.at[1:32], r.b_sem.at[1])
    for hop in range(1, 32):
        mean = mean + r.blocks[hop]
    count = pltpu.roll(mean, 32, 1)
    mean = mean + pltpu.roll(mean, 96, 1) + pltpu.roll(mean, 64, 1)
    mean = (mean / jnp.maximum(count, 1.0)).T
    star_ref[0] = mean[0:16]
    star_ref[1] = mean[16:32]
    total(r.g.at[:, :, x, zh, y], r.z_sem.at[0])
    total(r.g.at[:, :, 0:3, :, 0], r.p_sem.at[0])
    total(r.g.at[:, :, :, :, 0:3], r.g_send.at[0])
    total(r.u.at[0:7], r.u_send.at[0])
    total(r.e.at[0:7], r.e_send.at[0])
    total(r.part.at[0:7], r.a_sem.at[0])
    total(r.blocks.at[1:32], r.b_sem.at[0])


def local(g_real, lattice, u_rot, energy, band_mask, freq, froh, kq_index, irr_id):
    anywhere = pl.BlockSpec(memory_space=pl.ANY)
    vm = pl.BlockSpec(memory_space=pltpu.VMEM)
    scratch = {**scratch_shapes(), **io_shapes(), **semaphores()}
    return pl.pallas_call(
        functools.partial(kernel, list(scratch)),
        out_shape=(jax.ShapeDtypeStruct((2, 16, 128), F32), jax.ShapeDtypeStruct((2, 16, 16), F32)),
        in_specs=[anywhere] * 9,
        out_specs=(vm, vm),
        scratch_shapes=list(scratch.values()),
        compiler_params=pltpu.CompilerParams(collective_id=0, has_side_effects=True,
                                             vmem_limit_bytes=60 * 2 ** 20),
    )(g_real, u_rot.reshape(512, 128), energy, band_mask, lattice, kq_index, irr_id.reshape(1, 128), freq, froh)


def solution(mesh):
    in_specs = (
        P(None, "kp", None),
        P(),
        P(None, None, None, ("grp", "kp")),
        P(None, ("grp", "kp")),
        P(None, ("grp", "kp")),
        P(),
        P(),
        P(),
        P(("grp", "kp")),
    )
    out_specs = (P(None, None, ("grp", "kp")), P(None, None, ("grp", "kp")))
    return jax.shard_map(local, mesh=mesh, in_specs=in_specs, out_specs=out_specs, check_vma=False)
```

```python
import functools
import math
from types import SimpleNamespace

import jax
import jax.numpy as jnp
from jax import lax
from jax.experimental import pallas as pl
from jax.experimental.pallas import tpu as pltpu
from jax.sharding import PartitionSpec as P

KT = 0.025
ETA = 0.05
NKM = 40
F32, BF16 = jnp.float32, jnp.bfloat16
NT = (((1,), (1,)), ((), ()))
MESH = pl.DeviceIdType.MESH


def mod_mesh(values):
    return values - NKM * jnp.floor((values + 0.5) * (1.0 / NKM))


def turn(steps):
    x = (steps - 20.0) * (1.0 / 20.0)
    y = x * x
    cos, sin = 0.0, 0.0
    for n in range(8, -1, -1):
        cos = cos * y + (-1.0) ** n * math.pi ** (2 * n) / math.factorial(2 * n)
        sin = sin * y + (-1.0) ** n * math.pi ** (2 * n + 1) / math.factorial(2 * n + 1)
    return -cos, -(sin * x)


def pieces(x, count):
    out = []
    for _ in range(count):
        head = x.astype(BF16)
        out.append(head)
        x = x - head.astype(F32)
    return out


def dot(a, b):
    return jnp.dot(a, b, preferred_element_type=F32)


def dot_nt(a, b):
    return lax.dot_general(a, b, NT, preferred_element_type=F32)


def iota(shape, axis):
    return lax.broadcasted_iota(jnp.int32, shape, axis)


def together(work):
    while work:
        work = [w for w in work if next(w, work) is not work]


def swap_groups(parts):
    parts = list(parts)
    lane = iota(parts[0].shape, 1)
    for bit in (1, 2, 4):
        mask = (lane & (16 * bit)) != 0
        for low in range(8):
            if low & bit == 0:
                a, b = parts[low], parts[low | bit]
                parts[low] = jnp.where(mask, pltpu.roll(b, 16 * bit, 1), a)
                parts[low | bit] = jnp.where(mask, b, pltpu.roll(a, 128 - 16 * bit, 1))
    return parts


def scratch_shapes():
    vm = pltpu.VMEM
    return dict(
        g=vm((3, 2, 4, 2, 4, 32, 256), BF16),
        u=vm((8, 512, 128), BF16),
        e=vm((8, 32, 128), F32),
        ac=vm((40, 1024), F32), as_=vm((40, 1024), F32),
        bc=vm((128, 1024), F32), bs=vm((128, 1024), F32),
        ph=vm((8, 256, 2048), BF16),
        v=vm((2, 1024, 256), BF16),
        xs=vm((2, 8, 2, 256, 128), BF16),
        t1=vm((8, 3, 256, 256), BF16),
        t2=vm((2, 6, 128, 256), BF16),
        t3=vm((2, 6, 256, 128), BF16),
        ex=vm((128, 2048), F32), fa=vm((64, 2048), F32),
        sums=vm((256, 2048), F32),
        rep=vm((128, 2048), BF16), rept=vm((2048, 128), BF16), diag=vm((128, 128), BF16), eye=vm((128, 128), BF16),
        mix=vm((256, 256), BF16), perm=vm((128, 128), BF16), turned=vm((128, 128), BF16),
    )


def constants(r):
    rr, rl = iota((128, 2048), 0), iota((128, 2048), 1)
    r.rep[...] = jnp.where(rl // 16 == rr, 1.0, 0.0).astype(BF16)
    rr, rl = iota((2048, 128), 0), iota((2048, 128), 1)
    r.rept[...] = jnp.where(rr // 16 == rl, 1.0, 0.0).astype(BF16)
    sr, sl = iota((128, 128), 0), iota((128, 128), 1)
    r.diag[...] = jnp.where(sr // 16 == sl // 16, 1.0, 0.0).astype(BF16)
    br, bl = iota((256, 256), 0), iota((256, 256), 1)
    r.eye[...] = jnp.where(sr == sl, 1.0, 0.0).astype(BF16)
    r.mix[...] = jnp.where((br // 16 == bl % 16) & (br % 16 == bl // 16), 1.0, 0.0).astype(BF16)


def partner_order(r, kq, step):
    sr, sl = iota((128, 128), 0), iota((128, 128), 1)
    order = jnp.where(step == 0, kq[0:1, :], kq[1:2, :])
    perm = jnp.where(sr == order, 1.0, 0.0).T.astype(BF16)
    r.perm[...] = perm
    regroup = jnp.where((sr // 16 == sl % 8) & (sr % 16 == sl // 8), 1.0, 0.0).astype(BF16)
    r.turned[...] = dot(regroup, perm).astype(BF16)


def tables(r, lattice, first):
    lat = lattice.astype(F32)
    r.ac[...], r.as_[...] = turn(mod_mesh(iota((40, 1024), 0).astype(F32) * lat[0:1]))
    row16 = iota((16, 1024), 0).astype(F32)

    def one(s, carry):
        i0 = row16 * 8.0 + first(s).astype(F32) + 0.5
        n2 = mod_mesh(jnp.floor(i0 * (1.0 / 40.0)))
        n3 = mod_mesh(jnp.floor(i0 * (1.0 / 1600.0)))
        rows = pl.ds(pl.multiple_of(s * 16, 16), 16)
        r.bc[rows], r.bs[rows] = turn(mod_mesh(n2 * lat[1:2] + n3 * lat[2:3]))
        return carry

    lax.fori_loop(0, 8, one, 0)


def phases(r, s, first):
    base = first(s)

    def pair(o2, carry):
        cs, sn = [], []
        for h in range(2):
            o = o2 * 2 + h
            rows = pl.ds(pl.multiple_of(lax.rem(base + o * 8, NKM), 8), 8)
            a_c, a_s = r.ac[rows], r.as_[rows]
            b_c, b_s = r.bc[pl.ds(s * 16 + o, 1)], r.bs[pl.ds(s * 16 + o, 1)]
            cs.append(a_c * b_c - a_s * b_s)
            sn.append(a_s * b_c + a_c * b_s)
        co = jnp.concatenate(cs, 0).astype(BF16)
        si = jnp.concatenate(sn, 0)
        up = pl.ds(pl.multiple_of(o2 * 16, 16), 16)
        low = pl.ds(pl.multiple_of(o2 * 16 + 128, 16), 16)
        r.ph[s, up, 0:1024] = co
        r.ph[s, up, 1024:2048] = (-si).astype(BF16)
        r.ph[s, low, 0:1024] = si.astype(BF16)
        r.ph[s, low, 1024:2048] = co
        return carry

    lax.fori_loop(0, 8, pair, 0)


def partner_of(slot, step):
    return slot // 4 * 4 + lax.rem(lax.rem(slot, 4) + 7 - step, 4)


def levels(r, slot, step):
    own = pieces(r.e[slot, 0:16], 3)
    moved = dot_nt(jnp.concatenate(own + [r.e[slot, 16:32].astype(BF16)], 0), r.perm[...]).astype(BF16)
    yield
    both = dot(jnp.concatenate(own + [moved], 0), r.rep[...])
    yield
    r.ex[pl.ds(pl.multiple_of(slot * 16, 16), 16)] = both[0:16] + both[16:32] + both[32:48]
    pick = iota((16, 2048), 0) == iota((16, 2048), 1) % 16
    fe = jnp.where(pick, both[48:64] + both[64:80] + both[80:96], 0.0).sum(0, keepdims=True)
    fm = jnp.where(pick, both[96:112], 0.0).sum(0, keepdims=True)
    occ = 1.0 / (jnp.exp(fe * (1.0 / KT)) + 1.0)
    rows = pl.ds(pl.multiple_of(partner_of(slot, step) * 8, 8), 8)
    r.fa[rows] = jnp.concatenate([fe, fm, occ, jnp.zeros((5, 2048), F32)], 0)


def regroup_columns(tiles):
    cols = []
    for c in range(2):
        rows = []
        for hi in range(2):
            t = tiles[c][hi]
            rows += swap_groups([t[k * 16:k * 16 + 16] for k in range(8)])
        cols.append(jnp.concatenate(rows, 0))
    return jnp.concatenate(cols, 1)


def regroup_rows(r, tiles):
    return dot(r.mix[...], regroup_columns(tiles)).astype(BF16)


def rotations(r, w, slot, step):
    left, s = (r.eye[...], slot) if w == 0 else (r.turned[...], partner_of(slot, step))
    points = dot_nt(left, r.u[slot]).astype(BF16)
    yield
    cols = regroup_columns([[points[:, c * 256 + hi * 128:c * 256 + hi * 128 + 128] for hi in range(2)]
                            for c in range(2)])
    yield
    out = dot(r.mix[...], cols).astype(BF16)
    r.xs[w, s, 0] = out[:, 0:128]
    r.xs[w, s, 1] = out[:, 128:256]


def vertex(r, m, half, onsite):
    rows = r.ph[half * 4:half * 4 + 4].reshape(1024, 2048)
    v = dot(rows, r.g[m].reshape(2048, 256))
    for s in range(4):
        for c in range(2):
            at = s * 256 + c * 128
            r.v[half, at:at + 128] = (v[at:at + 128] + onsite[c]).astype(BF16)


def regroup_vertex(r, m, half):
    for s in range(4):
        parts = [[r.v[half, s * 256 + c * 128:s * 256 + c * 128 + 128, hi * 128:hi * 128 + 128] for hi in range(2)]
                 for c in range(2)]
        r.t1[half * 4 + s, m] = regroup_rows(r, parts)


def block_matrix(r, w, s, o):
    rows = slice(o * 16, o * 16 + 16)
    d = r.diag[...]
    return jnp.concatenate([jnp.concatenate([r.xs[w, s, i, rows]] * 8, 0) * d for i in range(2)], 1)


def self_energy(r, s, lane, bose, phonon):
    for o in range(16):
        rows = slice(o * 16, o * 16 + 16)
        left = jnp.concatenate([r.t1[s, m, rows, c * 128:c * 128 + 128] for c in range(2) for m in range(3)], 0)
        both = dot(left, block_matrix(r, 0, s, o))
        re = (both[0:48, 0:128] - both[48:96, 128:256]).astype(BF16)
        im = (both[0:48, 128:256] + both[48:96, 0:128]).astype(BF16)
        inner = slice(o % 8 * 16, o % 8 * 16 + 16)
        for m in range(3):
            r.t2[lane, o // 8 * 3 + m, inner, 0:128] = re[m * 16:m * 16 + 16]
            r.t2[lane, o // 8 * 3 + m, inner, 128:256] = im[m * 16:m * 16 + 16]
    yield
    for i in range(6):
        r.t3[lane, i] = r.t2[lane, i].T
    yield
    for o in range(16):
        hi, lo = o // 2, o % 2
        left = jnp.concatenate([r.t3[lane, lo * 3 + m, c * 128 + hi * 16:c * 128 + hi * 16 + 16]
                                for c in range(2) for m in range(3)], 0)
        both = dot(left, block_matrix(r, 1, s, o))
        br = both[0:48, 0:128] + both[48:96, 128:256]
        bi = both[48:96, 0:128] - both[0:48, 128:256]
        strength = br * br + bi * bi
        cols = slice(o * 128, o * 128 + 128)
        eo = r.ex[pl.ds(pl.multiple_of(s * 16, 16), 16), cols]
        far = r.fa[pl.ds(pl.multiple_of(s * 8, 8), 8), cols]
        fe, fm, occ = far[0:1], far[1:2], far[2:3]
        diff = eo - fe
        re, im = 0.0, 0.0
        for m in range(3):
            em = fm * (bose[m] + occ)
            ab = fm * (bose[m] + 1.0 - occ)
            up = diff + phonon[m]
            lw = diff - phonon[m]
            du = up * up + ETA * ETA
            dl = lw * lw + ETA * ETA
            scale = strength[m * 16:m * 16 + 16] / (du * dl)
            e1 = em * dl
            a1 = ab * du
            re = re + scale * (e1 * up + a1 * lw)
            im = im + scale * (e1 + a1)
        r.sums[pl.ds(pl.multiple_of(s * 32, 32), 16), cols] = re
        r.sums[pl.ds(pl.multiple_of(s * 32 + 16, 16), 16), cols] = im * (-ETA)


def band_sum(r):
    hi, lo = pieces(r.sums[...], 2)
    return (dot(hi, r.rept[...]) + dot(lo, r.rept[...])) * (1.0 / 384.0)


def mode_terms(freq, froh, step, mode0):
    lane = iota((1, 256), 1)
    site = jnp.where(lane // 16 == lane % 16, 1.0, 0.0)

    def pick(rows, m):
        row = jnp.where(step == 0, rows[0:1], rows[1:2])
        return jnp.where(iota((1, 12), 1) == mode0 + m, row, 0.0).sum(1, keepdims=True)

    onsite = [[site * pick(froh[:, c], m) for c in range(2)] for m in range(3)]
    phonon = [jnp.broadcast_to(pick(freq, m), (1, 128)) for m in range(3)]
    bose = [1.0 / (jnp.exp(w * (1.0 / KT)) - 1.0) for w in phonon]
    return onsite, phonon, bose


def loop(body, count=8):
    def step(s, carry):
        body(s)
        return carry
    lax.fori_loop(0, count, step, 0)


def position():
    kp = lax.axis_index("kp")
    return lax.axis_index("grp"), kp // 8, kp // 4 % 2, kp % 4


def at(g, x, zh, y):
    return (g, x * 8 + zh * 4 + y)


def column(g, zh):
    for hop in range(1, 8):
        other = (zh * 4 + g + hop) % 8
        yield hop, other % 4, other // 4


def remote(src, dst, send, recv, device):
    return pltpu.make_async_remote_copy(src_ref=src, dst_ref=dst, send_sem=send, recv_sem=recv,
                                        device_id=device, device_id_type=MESH)


def semaphores():
    dma = pltpu.SemaphoreType.DMA
    return dict(
        in_sem=dma((8,)), near_sem=dma((1,)), z_sem=dma((2,)), p_sem=dma((2,)), g_send=dma((1,)), g_recv=dma((3,)),
        u_send=dma((1,)), u_recv=dma((8,)), e_send=dma((1,)), e_recv=dma((8,)), a_sem=dma((2,)), b_sem=dma((2,)),
    )


def io_shapes():
    vm = pltpu.VMEM
    return dict(
        uin=vm((512, 128), F32), en=vm((16, 128), F32), mask=vm((16, 128), jnp.int32),
        lat=vm((3, 1024), jnp.int32), kq=vm((2, 128), jnp.int32), irr=vm((1, 128), jnp.int32),
        part=vm((8, 32, 128), F32), got=vm((8, 32, 128), F32),
        stars=vm((512, 128), F32), blocks=vm((32, 16, 128), F32),
        freq=vm((2, 12), F32), froh=vm((2, 2, 12), F32),
    )


def kernel(names, g_ref, u_ref, en_ref, mask_ref, lat_ref, kq_ref, irr_ref, freq_ref, froh_ref,
           sigma_ref, star_ref, *scratch):
    r = SimpleNamespace(**dict(zip(names, scratch)))
    g, x, zh, y = position()
    me = x * 8 + zh * 4 + y
    mine = zh * 4 + g
    step, mode0 = zh, g * 3

    def first(s):
        return (x * 8 + y) * 128 + lax.rem(s, 4) * 4096 + s // 4 * 512

    loads = [pltpu.make_async_copy(src, dst, r.in_sem.at[i]) for i, (src, dst) in enumerate(
        ((u_ref, r.uin), (en_ref, r.en), (mask_ref, r.mask), (lat_ref, r.lat), (kq_ref, r.kq), (irr_ref, r.irr),
         (freq_ref, r.freq), (froh_ref, r.froh)))]
    for copy in loads:
        copy.start()

    barrier = pltpu.get_barrier_semaphore()
    friends = [at(g2, x, zh2, y) for _, g2, zh2 in column(g, zh)] + [(g, (me + hop) % 32) for hop in range(1, 32)]
    for device in friends:
        pl.semaphore_signal(barrier, inc=1, device_id=device, device_id_type=MESH)

    def part(at_step, triple, c, m):
        return g_ref.at[at_step, :, pl.ds(pl.multiple_of(c * 3072 + triple * 768 + m * 256, 256), 256)]

    for c in range(2):
        for m in range(3):
            pltpu.make_async_copy(part(zh, g, c, m), r.g.at[m, c, x, zh, y], r.near_sem.at[0]).start()
    pl.semaphore_wait(barrier, len(friends))

    pz, pg = 1 - zh, (g + 2) % 4
    for c in range(2):
        for m in range(3):
            remote(part(pz, pg, c, m), r.g.at[m, c, x, zh, y], r.z_sem.at[0], r.z_sem.at[1], at(pg, x, pz, y)).start()

    def total(ref, sem):
        pltpu.make_async_copy(ref, ref, sem).wait()

    def plane(hop, along_x):
        return at(g, (x + hop) % 4, zh, y) if along_x else at(g, x, zh, (y + hop) % 4)

    def first_leg(c, z):
        piece = r.g.at[:, c, x, z, y]
        for hop in (1, 3, 2):
            remote(piece, piece, r.p_sem.at[0], r.p_sem.at[1], plane(hop, c == 0)).start()

    total(r.g.at[:, :, x, zh, y], r.near_sem.at[0])
    for c in range(2):
        first_leg(c, zh)

    chip, sibling = mine // 2, at(g // 2 * 2 + 1 - g % 2, x, zh, y)

    def share(slot, sem, device):
        for buf, send, recv in ((r.u, r.u_send, r.u_recv), (r.e, r.e_send, r.e_recv)):
            remote(buf.at[slot], buf.at[slot], send.at[0], recv.at[sem], device).start()

    def shared(slot, sem):
        for buf, send, recv in ((r.u, r.u_send, r.u_recv), (r.e, r.e_send, r.e_recv)):
            total(buf.at[slot], recv.at[sem])

    for i in range(3):
        loads[i].wait()
    r.u[mine] = r.uin[...].astype(BF16)
    r.e[mine, 0:16] = r.en[...]
    r.e[mine, 16:32] = r.mask[...].astype(F32)
    for hop in (1, 3, 2):
        to = (chip + hop) % 4
        share(mine, hop, at(to % 2 * 2 + g % 2, x, to // 2, y))
    share(mine, 0, sibling)

    constants(r)
    loads[4].wait()
    partner_order(r, r.kq[...], step)
    total(r.g.at[:, :, x, pz, y], r.z_sem.at[1])
    for c in range(2):
        first_leg(c, 1 - zh)

    def second_leg(m, c, hop):
        xs, ys = ((x + 4 - hop) % 4, y) if c == 0 else (x, (y + 4 - hop) % 4)
        piece = r.g.at[m, c, xs, :, ys]
        for to in (1, 3, 2):
            remote(piece, piece, r.g_send.at[0], r.g_recv.at[m], plane(to, c == 1)).start()

    for c in range(2):
        second_leg(0, c, 0)
    loads[3].wait()
    tables(r, r.lat[...], first)
    total(r.g.at[:, :, 0:3, :, 0], r.p_sem.at[1])
    for m in range(3):
        for hop in (0, 1, 3, 2):
            for c in range(2):
                if m or hop:
                    second_leg(m, c, hop)
    loop(lambda s: phases(r, s, first))

    def there(hop):
        return (chip + 4 - hop) % 4

    def forward(hop):
        shared(there(hop) * 2 + g % 2, hop)
        share(there(hop) * 2 + g % 2, 4 + hop, sibling)

    def prepare(hop):
        shared(there(hop) * 2 + 1 - g % 2, 4 + hop if hop else 0)
        slots = [there(hop) * 2, there(hop) * 2 + 1]
        together([rotations(r, w, slot, step) for slot in slots for w in range(2)]
                 + [levels(r, slot, step) for slot in slots])

    forward(1)
    prepare(0)
    forward(3)
    forward(2)
    prepare(1)
    prepare(3)
    prepare(2)
    loads[6].wait()
    loads[7].wait()
    onsite, phonon, bose = mode_terms(r.freq[...], r.froh[...], step, mode0)

    for m in range(3):
        total(r.g.at[m, :, :, :, 0:3], r.g_recv.at[m])
        vertex(r, m, 0, onsite[m])
        if m:
            regroup_vertex(r, m - 1, 1)
        vertex(r, m, 1, onsite[m])
        regroup_vertex(r, m, 0)
    regroup_vertex(r, 2, 1)
    loop(lambda i: together([self_energy(r, 2 * i + q, q, bose, phonon) for q in range(2)]), 4)
    sums = band_sum(r)
    for s in range(8):
        r.part[s] = sums[s * 32:s * 32 + 32]

    for hop, g2, zh2 in column(g, zh):
        remote(r.part.at[zh2 * 4 + g2], r.got.at[hop], r.a_sem.at[0], r.a_sem.at[1], at(g2, x, zh2, y)).start()
    loads[5].wait()
    member = jnp.where(iota((512, 128), 0) == r.irr[...], 1.0, 0.0).astype(BF16)
    total(r.got.at[1:8], r.a_sem.at[1])
    sigma = r.part[mine]
    for hop in range(1, 8):
        sigma = sigma + r.got[hop]
    sigma_ref[0] = sigma[0:16]
    sigma_ref[1] = sigma[16:32]
    columns = jnp.concatenate(pieces(sigma, 3) + [jnp.ones((32, 128), BF16)], 0)
    r.stars[...] = dot_nt(member, columns)
    for hop in range(1, 32):
        owner = (me + hop) % 32
        remote(r.stars.at[pl.ds(pl.multiple_of(owner * 16, 16), 16)], r.blocks.at[hop],
               r.b_sem.at[0], r.b_sem.at[1], (g, owner)).start()
    mean = r.stars[pl.ds(pl.multiple_of(me * 16, 16), 16)]
    total(r.blocks.at[1:32], r.b_sem.at[1])
    for hop in range(1, 32):
        mean = mean + r.blocks[hop]
    count = pltpu.roll(mean, 32, 1)
    mean = mean + pltpu.roll(mean, 96, 1) + pltpu.roll(mean, 64, 1)
    mean = (mean / jnp.maximum(count, 1.0)).T
    star_ref[0] = mean[0:16]
    star_ref[1] = mean[16:32]
    total(r.g.at[:, :, x, zh, y], r.z_sem.at[0])
    total(r.g.at[:, :, 0:3, :, 0], r.p_sem.at[0])
    total(r.g.at[:, :, :, :, 0:3], r.g_send.at[0])
    total(r.u.at[0:7], r.u_send.at[0])
    total(r.e.at[0:7], r.e_send.at[0])
    total(r.part.at[0:7], r.a_sem.at[0])
    total(r.blocks.at[1:32], r.b_sem.at[0])


def local(g_real, lattice, u_rot, energy, band_mask, freq, froh, kq_index, irr_id):
    anywhere = pl.BlockSpec(memory_space=pl.ANY)
    vm = pl.BlockSpec(memory_space=pltpu.VMEM)
    scratch = {**scratch_shapes(), **io_shapes(), **semaphores()}
    results = pl.pallas_call(
        functools.partial(kernel, list(scratch)),
        out_shape=(jax.ShapeDtypeStruct((2, 16, 128), F32), jax.ShapeDtypeStruct((2, 16, 16), F32)),
        in_specs=[anywhere] * 9,
        out_specs=(vm, vm),
        scratch_shapes=list(scratch.values()),
        compiler_params=pltpu.CompilerParams(collective_id=0, has_side_effects=True,
                                             vmem_limit_bytes=60 * 2 ** 20),
    )(g_real, u_rot.reshape(512, 128), energy, band_mask, lattice, kq_index, irr_id.reshape(1, 128), freq, froh)


    def hand_over(sigma_ref, star_ref, sigma_out, star_out):
        sigma_out[...] = sigma_ref[...]
        star_out[...] = star_ref[...]

    return pl.pallas_call(
        hand_over,
        out_shape=(jax.ShapeDtypeStruct((2, 16, 128), F32), jax.ShapeDtypeStruct((2, 16, 16), F32)),
        in_specs=[vm, vm],
        out_specs=(vm, vm),
    )(*results)


def solution(mesh):
    in_specs = (
        P(None, "kp", None),
        P(),
        P(None, None, None, ("grp", "kp")),
        P(None, ("grp", "kp")),
        P(None, ("grp", "kp")),
        P(),
        P(),
        P(),
        P(("grp", "kp")),
    )
    out_specs = (P(None, None, ("grp", "kp")), P(None, None, ("grp", "kp")))
    return jax.shard_map(local, mesh=mesh, in_specs=in_specs, out_specs=out_specs, check_vma=False)
```

```python
import functools
import math
from types import SimpleNamespace

import jax
import jax.numpy as jnp
from jax import lax
from jax.experimental import pallas as pl
from jax.experimental.pallas import tpu as pltpu
from jax.sharding import PartitionSpec as P

KT = 0.025
ETA = 0.05
NKM = 40
F32, BF16 = jnp.float32, jnp.bfloat16
NT = (((1,), (1,)), ((), ()))
MESH = pl.DeviceIdType.MESH


def mod_mesh(values):
    return values - NKM * jnp.floor((values + 0.5) * (1.0 / NKM))


def turn(steps):
    x = (steps - 20.0) * (1.0 / 20.0)
    y = x * x
    cos, sin = 0.0, 0.0
    for n in range(8, -1, -1):
        cos = cos * y + (-1.0) ** n * math.pi ** (2 * n) / math.factorial(2 * n)
        sin = sin * y + (-1.0) ** n * math.pi ** (2 * n + 1) / math.factorial(2 * n + 1)
    return -cos, -(sin * x)


def pieces(x, count):
    out = []
    for _ in range(count):
        head = x.astype(BF16)
        out.append(head)
        x = x - head.astype(F32)
    return out


def dot(a, b):
    return jnp.dot(a, b, preferred_element_type=F32)


def dot_nt(a, b):
    return lax.dot_general(a, b, NT, preferred_element_type=F32)


def iota(shape, axis):
    return lax.broadcasted_iota(jnp.int32, shape, axis)


def together(work):
    while work:
        work = [w for w in work if next(w, work) is not work]


def swap_groups(parts):
    parts = list(parts)
    lane = iota(parts[0].shape, 1)
    for bit in (1, 2, 4):
        mask = (lane & (16 * bit)) != 0
        for low in range(8):
            if low & bit == 0:
                a, b = parts[low], parts[low | bit]
                parts[low] = jnp.where(mask, pltpu.roll(b, 16 * bit, 1), a)
                parts[low | bit] = jnp.where(mask, b, pltpu.roll(a, 128 - 16 * bit, 1))
    return parts


def scratch_shapes():
    vm = pltpu.VMEM
    return dict(
        g=vm((3, 2, 4, 2, 4, 32, 256), BF16),
        u=vm((8, 512, 128), BF16),
        e=vm((8, 32, 128), F32),
        ac=vm((40, 1024), F32), as_=vm((40, 1024), F32),
        bc=vm((128, 1024), F32), bs=vm((128, 1024), F32),
        ph=vm((8, 256, 2048), BF16),
        v=vm((2, 1024, 256), BF16),
        xs=vm((2, 8, 2, 256, 128), BF16),
        t1=vm((8, 3, 256, 256), BF16),
        t2=vm((2, 6, 128, 256), BF16),
        t3=vm((2, 6, 256, 128), BF16),
        ex=vm((128, 2048), F32), fa=vm((64, 2048), F32),
        sums=vm((256, 2048), F32),
        rep=vm((128, 2048), BF16), rept=vm((2048, 128), BF16), diag=vm((128, 128), BF16), eye=vm((128, 128), BF16),
        mix=vm((256, 256), BF16), perm=vm((128, 128), BF16), turned=vm((128, 128), BF16),
    )


def constants(r):
    rr, rl = iota((128, 2048), 0), iota((128, 2048), 1)
    r.rep[...] = jnp.where(rl // 16 == rr, 1.0, 0.0).astype(BF16)
    rr, rl = iota((2048, 128), 0), iota((2048, 128), 1)
    r.rept[...] = jnp.where(rr // 16 == rl, 1.0, 0.0).astype(BF16)
    sr, sl = iota((128, 128), 0), iota((128, 128), 1)
    r.diag[...] = jnp.where(sr // 16 == sl // 16, 1.0, 0.0).astype(BF16)
    br, bl = iota((256, 256), 0), iota((256, 256), 1)
    r.eye[...] = jnp.where(sr == sl, 1.0, 0.0).astype(BF16)
    r.mix[...] = jnp.where((br // 16 == bl % 16) & (br % 16 == bl // 16), 1.0, 0.0).astype(BF16)


def partner_order(r, kq, step):
    sr, sl = iota((128, 128), 0), iota((128, 128), 1)
    order = jnp.where(step == 0, kq[0:1, :], kq[1:2, :])
    perm = jnp.where(sr == order, 1.0, 0.0).T.astype(BF16)
    r.perm[...] = perm
    regroup = jnp.where((sr // 16 == sl % 8) & (sr % 16 == sl // 8), 1.0, 0.0).astype(BF16)
    r.turned[...] = dot(regroup, perm).astype(BF16)


def tables(r, lattice, first):
    lat = lattice.astype(F32)
    r.ac[...], r.as_[...] = turn(mod_mesh(iota((40, 1024), 0).astype(F32) * lat[0:1]))
    row16 = iota((16, 1024), 0).astype(F32)

    def one(s, carry):
        i0 = row16 * 8.0 + first(s).astype(F32) + 0.5
        n2 = mod_mesh(jnp.floor(i0 * (1.0 / 40.0)))
        n3 = mod_mesh(jnp.floor(i0 * (1.0 / 1600.0)))
        rows = pl.ds(pl.multiple_of(s * 16, 16), 16)
        r.bc[rows], r.bs[rows] = turn(mod_mesh(n2 * lat[1:2] + n3 * lat[2:3]))
        return carry

    lax.fori_loop(0, 8, one, 0)


def phases(r, s, first):
    base = first(s)

    def pair(o2, carry):
        cs, sn = [], []
        for h in range(2):
            o = o2 * 2 + h
            rows = pl.ds(pl.multiple_of(lax.rem(base + o * 8, NKM), 8), 8)
            a_c, a_s = r.ac[rows], r.as_[rows]
            b_c, b_s = r.bc[pl.ds(s * 16 + o, 1)], r.bs[pl.ds(s * 16 + o, 1)]
            cs.append(a_c * b_c - a_s * b_s)
            sn.append(a_s * b_c + a_c * b_s)
        co = jnp.concatenate(cs, 0).astype(BF16)
        si = jnp.concatenate(sn, 0)
        up = pl.ds(pl.multiple_of(o2 * 16, 16), 16)
        low = pl.ds(pl.multiple_of(o2 * 16 + 128, 16), 16)
        r.ph[s, up, 0:1024] = co
        r.ph[s, up, 1024:2048] = (-si).astype(BF16)
        r.ph[s, low, 0:1024] = si.astype(BF16)
        r.ph[s, low, 1024:2048] = co
        return carry

    lax.fori_loop(0, 8, pair, 0)


def partner_of(slot, step):
    return slot // 4 * 4 + lax.rem(lax.rem(slot, 4) + 7 - step, 4)


def levels(r, slot, step):
    own = pieces(r.e[slot, 0:16], 3)
    moved = dot_nt(jnp.concatenate(own + [r.e[slot, 16:32].astype(BF16)], 0), r.perm[...]).astype(BF16)
    yield
    both = dot(jnp.concatenate(own + [moved], 0), r.rep[...])
    yield
    r.ex[pl.ds(pl.multiple_of(slot * 16, 16), 16)] = both[0:16] + both[16:32] + both[32:48]
    pick = iota((16, 2048), 0) == iota((16, 2048), 1) % 16
    fe = jnp.where(pick, both[48:64] + both[64:80] + both[80:96], 0.0).sum(0, keepdims=True)
    fm = jnp.where(pick, both[96:112], 0.0).sum(0, keepdims=True)
    occ = 1.0 / (jnp.exp(fe * (1.0 / KT)) + 1.0)
    rows = pl.ds(pl.multiple_of(partner_of(slot, step) * 8, 8), 8)
    r.fa[rows] = jnp.concatenate([fe, fm, occ, jnp.zeros((5, 2048), F32)], 0)


def regroup_columns(tiles):
    cols = []
    for c in range(2):
        rows = []
        for hi in range(2):
            t = tiles[c][hi]
            rows += swap_groups([t[k * 16:k * 16 + 16] for k in range(8)])
        cols.append(jnp.concatenate(rows, 0))
    return jnp.concatenate(cols, 1)


def regroup_rows(r, tiles):
    return dot(r.mix[...], regroup_columns(tiles)).astype(BF16)


def rotations(r, w, slot, step):
    left, s = (r.eye[...], slot) if w == 0 else (r.turned[...], partner_of(slot, step))
    points = dot_nt(left, r.u[slot]).astype(BF16)
    yield
    cols = regroup_columns([[points[:, c * 256 + hi * 128:c * 256 + hi * 128 + 128] for hi in range(2)]
                            for c in range(2)])
    yield
    out = dot(r.mix[...], cols).astype(BF16)
    r.xs[w, s, 0] = out[:, 0:128]
    r.xs[w, s, 1] = out[:, 128:256]


def vertex(r, m, half, onsite):
    rows = r.ph[half * 4:half * 4 + 4].reshape(1024, 2048)
    v = dot(rows, r.g[m].reshape(2048, 256))
    for s in range(4):
        for c in range(2):
            at = s * 256 + c * 128
            r.v[half, at:at + 128] = (v[at:at + 128] + onsite[c]).astype(BF16)


def regroup_vertex(r, m, half):
    for s in range(4):
        parts = [[r.v[half, s * 256 + c * 128:s * 256 + c * 128 + 128, hi * 128:hi * 128 + 128] for hi in range(2)]
                 for c in range(2)]
        r.t1[half * 4 + s, m] = regroup_rows(r, parts)


def block_matrix(r, w, s, o):
    rows = slice(o * 16, o * 16 + 16)
    d = r.diag[...]
    return jnp.concatenate([jnp.concatenate([r.xs[w, s, i, rows]] * 8, 0) * d for i in range(2)], 1)


def self_energy(r, s, lane, bose, phonon):
    for o in range(16):
        rows = slice(o * 16, o * 16 + 16)
        left = jnp.concatenate([r.t1[s, m, rows, c * 128:c * 128 + 128] for c in range(2) for m in range(3)], 0)
        both = dot(left, block_matrix(r, 0, s, o))
        re = (both[0:48, 0:128] - both[48:96, 128:256]).astype(BF16)
        im = (both[0:48, 128:256] + both[48:96, 0:128]).astype(BF16)
        inner = slice(o % 8 * 16, o % 8 * 16 + 16)
        for m in range(3):
            r.t2[lane, o // 8 * 3 + m, inner, 0:128] = re[m * 16:m * 16 + 16]
            r.t2[lane, o // 8 * 3 + m, inner, 128:256] = im[m * 16:m * 16 + 16]
    yield
    for i in range(6):
        r.t3[lane, i] = r.t2[lane, i].T
    yield
    for o in range(16):
        hi, lo = o // 2, o % 2
        left = jnp.concatenate([r.t3[lane, lo * 3 + m, c * 128 + hi * 16:c * 128 + hi * 16 + 16]
                                for c in range(2) for m in range(3)], 0)
        both = dot(left, block_matrix(r, 1, s, o))
        br = both[0:48, 0:128] + both[48:96, 128:256]
        bi = both[48:96, 0:128] - both[0:48, 128:256]
        strength = br * br + bi * bi
        cols = slice(o * 128, o * 128 + 128)
        eo = r.ex[pl.ds(pl.multiple_of(s * 16, 16), 16), cols]
        far = r.fa[pl.ds(pl.multiple_of(s * 8, 8), 8), cols]
        fe, fm, occ = far[0:1], far[1:2], far[2:3]
        diff = eo - fe
        re, im = 0.0, 0.0
        for m in range(3):
            em = fm * (bose[m] + occ)
            ab = fm * (bose[m] + 1.0 - occ)
            up = diff + phonon[m]
            lw = diff - phonon[m]
            du = up * up + ETA * ETA
            dl = lw * lw + ETA * ETA
            scale = strength[m * 16:m * 16 + 16] / (du * dl)
            e1 = em * dl
            a1 = ab * du
            re = re + scale * (e1 * up + a1 * lw)
            im = im + scale * (e1 + a1)
        r.sums[pl.ds(pl.multiple_of(s * 32, 32), 16), cols] = re
        r.sums[pl.ds(pl.multiple_of(s * 32 + 16, 16), 16), cols] = im * (-ETA)


def band_sum(r, half):
    hi, lo = pieces(r.sums[half * 128:half * 128 + 128], 2)
    return (dot(hi, r.rept[...]) + dot(lo, r.rept[...])) * (1.0 / 384.0)


def mode_terms(freq, froh, step, mode0):
    lane = iota((1, 256), 1)
    site = jnp.where(lane // 16 == lane % 16, 1.0, 0.0)

    def pick(rows, m):
        row = jnp.where(step == 0, rows[0:1], rows[1:2])
        return jnp.where(iota((1, 12), 1) == mode0 + m, row, 0.0).sum(1, keepdims=True)

    onsite = [[site * pick(froh[:, c], m) for c in range(2)] for m in range(3)]
    phonon = [jnp.broadcast_to(pick(freq, m), (1, 128)) for m in range(3)]
    bose = [1.0 / (jnp.exp(w * (1.0 / KT)) - 1.0) for w in phonon]
    return onsite, phonon, bose


def loop(body, count=8):
    def step(s, carry):
        body(s)
        return carry
    lax.fori_loop(0, count, step, 0)


def position():
    kp = lax.axis_index("kp")
    return lax.axis_index("grp"), kp // 8, kp // 4 % 2, kp % 4


def at(g, x, zh, y):
    return (g, x * 8 + zh * 4 + y)


def column(g, zh):
    for hop in range(1, 8):
        other = (zh * 4 + g + hop) % 8
        yield hop, other % 4, other // 4


def remote(src, dst, send, recv, device):
    return pltpu.make_async_remote_copy(src_ref=src, dst_ref=dst, send_sem=send, recv_sem=recv,
                                        device_id=device, device_id_type=MESH)


def semaphores():
    dma = pltpu.SemaphoreType.DMA
    return dict(
        in_sem=dma((8,)), near_sem=dma((1,)), z_sem=dma((2,)), p_sem=dma((2,)), g_send=dma((1,)), g_recv=dma((3,)),
        u_send=dma((1,)), u_recv=dma((8,)), e_send=dma((1,)), e_recv=dma((8,)), a_sem=dma((2,)), b_sem=dma((2,)),
    )


def io_shapes():
    vm = pltpu.VMEM
    return dict(
        uin=vm((512, 128), F32), en=vm((16, 128), F32), mask=vm((16, 128), jnp.int32),
        lat=vm((3, 1024), jnp.int32), kq=vm((2, 128), jnp.int32), irr=vm((1, 128), jnp.int32),
        part=vm((8, 32, 128), F32), got=vm((8, 32, 128), F32),
        stars=vm((512, 128), F32), blocks=vm((32, 16, 128), F32),
        freq=vm((2, 12), F32), froh=vm((2, 2, 12), F32),
    )


def kernel(names, g_ref, u_ref, en_ref, mask_ref, lat_ref, kq_ref, irr_ref, freq_ref, froh_ref,
           sigma_ref, star_ref, *scratch):
    r = SimpleNamespace(**dict(zip(names, scratch)))
    g, x, zh, y = position()
    me = x * 8 + zh * 4 + y
    mine = zh * 4 + g
    step, mode0 = zh, g * 3

    def first(s):
        return (x * 8 + y) * 128 + lax.rem(s, 4) * 4096 + s // 4 * 512

    loads = [pltpu.make_async_copy(src, dst, r.in_sem.at[i]) for i, (src, dst) in enumerate(
        ((u_ref, r.uin), (en_ref, r.en), (mask_ref, r.mask), (lat_ref, r.lat), (kq_ref, r.kq), (irr_ref, r.irr),
         (freq_ref, r.freq), (froh_ref, r.froh)))]
    for copy in loads:
        copy.start()

    barrier = pltpu.get_barrier_semaphore()
    friends = [at(g2, x, zh2, y) for _, g2, zh2 in column(g, zh)] + [(g, (me + hop) % 32) for hop in range(1, 32)]
    for device in friends:
        pl.semaphore_signal(barrier, inc=1, device_id=device, device_id_type=MESH)

    def part(at_step, triple, c, m):
        return g_ref.at[at_step, :, pl.ds(pl.multiple_of(c * 3072 + triple * 768 + m * 256, 256), 256)]

    for c in range(2):
        for m in range(3):
            pltpu.make_async_copy(part(zh, g, c, m), r.g.at[m, c, x, zh, y], r.near_sem.at[0]).start()
    pl.semaphore_wait(barrier, len(friends))

    pz, pg = 1 - zh, (g + 2) % 4
    for c in range(2):
        for m in range(3):
            remote(part(pz, pg, c, m), r.g.at[m, c, x, zh, y], r.z_sem.at[0], r.z_sem.at[1], at(pg, x, pz, y)).start()

    def total(ref, sem):
        pltpu.make_async_copy(ref, ref, sem).wait()

    def plane(hop, along_x):
        return at(g, (x + hop) % 4, zh, y) if along_x else at(g, x, zh, (y + hop) % 4)

    def first_leg(c, z):
        piece = r.g.at[:, c, x, z, y]
        for hop in (1, 3, 2):
            remote(piece, piece, r.p_sem.at[0], r.p_sem.at[1], plane(hop, c == 0)).start()

    total(r.g.at[:, :, x, zh, y], r.near_sem.at[0])
    for c in range(2):
        first_leg(c, zh)

    chip, sibling = mine // 2, at(g // 2 * 2 + 1 - g % 2, x, zh, y)

    def share(slot, sem, device):
        for buf, send, recv in ((r.u, r.u_send, r.u_recv), (r.e, r.e_send, r.e_recv)):
            remote(buf.at[slot], buf.at[slot], send.at[0], recv.at[sem], device).start()

    def shared(slot, sem):
        for buf, send, recv in ((r.u, r.u_send, r.u_recv), (r.e, r.e_send, r.e_recv)):
            total(buf.at[slot], recv.at[sem])

    for i in range(3):
        loads[i].wait()
    r.u[mine] = r.uin[...].astype(BF16)
    r.e[mine, 0:16] = r.en[...]
    r.e[mine, 16:32] = r.mask[...].astype(F32)
    for hop in (1, 3, 2):
        to = (chip + hop) % 4
        share(mine, hop, at(to % 2 * 2 + g % 2, x, to // 2, y))
    share(mine, 0, sibling)

    constants(r)
    loads[4].wait()
    partner_order(r, r.kq[...], step)
    total(r.g.at[:, :, x, pz, y], r.z_sem.at[1])
    for c in range(2):
        first_leg(c, 1 - zh)

    def second_leg(m, c, hop):
        xs, ys = ((x + 4 - hop) % 4, y) if c == 0 else (x, (y + 4 - hop) % 4)
        piece = r.g.at[m, c, xs, :, ys]
        for to in (2, 1, 3):
            remote(piece, piece, r.g_send.at[0], r.g_recv.at[m], plane(to, c == 1)).start()

    for c in range(2):
        second_leg(0, c, 0)
    loads[3].wait()
    tables(r, r.lat[...], first)
    total(r.g.at[:, :, 0:3, :, 0], r.p_sem.at[1])
    for m in range(3):
        for hop in (0, 1, 3, 2):
            for c in range(2):
                if m or hop:
                    second_leg(m, c, hop)
    loop(lambda s: phases(r, s, first))

    def there(hop):
        return (chip + 4 - hop) % 4

    def forward(hop):
        shared(there(hop) * 2 + g % 2, hop)
        share(there(hop) * 2 + g % 2, 4 + hop, sibling)

    def prepare(hop):
        shared(there(hop) * 2 + 1 - g % 2, 4 + hop if hop else 0)
        slots = [there(hop) * 2, there(hop) * 2 + 1]
        together([rotations(r, w, slot, step) for slot in slots for w in range(2)]
                 + [levels(r, slot, step) for slot in slots])

    forward(1)
    prepare(0)
    forward(3)
    forward(2)
    prepare(1)
    prepare(3)
    prepare(2)
    loads[6].wait()
    loads[7].wait()
    onsite, phonon, bose = mode_terms(r.freq[...], r.froh[...], step, mode0)

    for m in range(3):
        total(r.g.at[m, :, :, :, 0:3], r.g_recv.at[m])
        vertex(r, m, 0, onsite[m])
        if m:
            regroup_vertex(r, m - 1, 1)
        vertex(r, m, 1, onsite[m])
        regroup_vertex(r, m, 0)
    regroup_vertex(r, 2, 1)
    def sums_of(half):
        sums = band_sum(r, half)
        for s in range(4):
            r.part[half * 4 + s] = sums[s * 32:s * 32 + 32]

    def to_owners(z):
        for g2 in range(4):
            slot = z * 4 + g2
            copy = remote(r.part.at[slot], r.got.at[mine], r.a_sem.at[0], r.a_sem.at[1], (g2, x * 8 + z * 4 + y))
            pl.when(slot != mine)(copy.start)

    loop(lambda i: together([self_energy(r, 2 * i + q, q, bose, phonon) for q in range(2)]), 2)
    sums_of(0)
    to_owners(0)
    loop(lambda i: together([self_energy(r, 2 * i + q + 4, q, bose, phonon) for q in range(2)]), 2)
    sums_of(1)
    to_owners(1)

    loads[5].wait()
    member = jnp.where(iota((512, 128), 0) == r.irr[...], 1.0, 0.0).astype(BF16)
    total(r.got.at[1:8], r.a_sem.at[1])
    r.got[mine] = r.part[mine]
    sigma = r.got[0]
    for slot in range(1, 8):
        sigma = sigma + r.got[slot]
    sigma_ref[0] = sigma[0:16]
    sigma_ref[1] = sigma[16:32]
    columns = jnp.concatenate(pieces(sigma, 3) + [jnp.ones((32, 128), BF16)], 0)
    r.stars[...] = dot_nt(member, columns)
    for hop in range(1, 32):
        owner = (me + hop) % 32
        remote(r.stars.at[pl.ds(pl.multiple_of(owner * 16, 16), 16)], r.blocks.at[hop],
               r.b_sem.at[0], r.b_sem.at[1], (g, owner)).start()
    mean = r.stars[pl.ds(pl.multiple_of(me * 16, 16), 16)]
    total(r.blocks.at[1:32], r.b_sem.at[1])
    for hop in range(1, 32):
        mean = mean + r.blocks[hop]
    count = pltpu.roll(mean, 32, 1)
    mean = mean + pltpu.roll(mean, 96, 1) + pltpu.roll(mean, 64, 1)
    mean = (mean / jnp.maximum(count, 1.0)).T
    star_ref[0] = mean[0:16]
    star_ref[1] = mean[16:32]
    total(r.g.at[:, :, x, zh, y], r.z_sem.at[0])
    total(r.g.at[:, :, 0:3, :, 0], r.p_sem.at[0])
    total(r.g.at[:, :, :, :, 0:3], r.g_send.at[0])
    total(r.u.at[0:7], r.u_send.at[0])
    total(r.e.at[0:7], r.e_send.at[0])
    total(r.part.at[0:7], r.a_sem.at[0])
    total(r.blocks.at[1:32], r.b_sem.at[0])


def local(g_real, lattice, u_rot, energy, band_mask, freq, froh, kq_index, irr_id):
    anywhere = pl.BlockSpec(memory_space=pl.ANY)
    vm = pl.BlockSpec(memory_space=pltpu.VMEM)
    scratch = {**scratch_shapes(), **io_shapes(), **semaphores()}
    results = pl.pallas_call(
        functools.partial(kernel, list(scratch)),
        out_shape=(jax.ShapeDtypeStruct((2, 16, 128), F32), jax.ShapeDtypeStruct((2, 16, 16), F32)),
        in_specs=[anywhere] * 9,
        out_specs=(vm, vm),
        scratch_shapes=list(scratch.values()),
        compiler_params=pltpu.CompilerParams(collective_id=0, has_side_effects=True,
                                             vmem_limit_bytes=60 * 2 ** 20),
    )(g_real, u_rot.reshape(512, 128), energy, band_mask, lattice, kq_index, irr_id.reshape(1, 128), freq, froh)


    def hand_over(sigma_ref, star_ref, sigma_out, star_out):
        sigma_out[...] = sigma_ref[...]
        star_out[...] = star_ref[...]

    return pl.pallas_call(
        hand_over,
        out_shape=(jax.ShapeDtypeStruct((2, 16, 128), F32), jax.ShapeDtypeStruct((2, 16, 16), F32)),
        in_specs=[vm, vm],
        out_specs=(vm, vm),
    )(*results)


def solution(mesh):
    in_specs = (
        P(None, "kp", None),
        P(),
        P(None, None, None, ("grp", "kp")),
        P(None, ("grp", "kp")),
        P(None, ("grp", "kp")),
        P(),
        P(),
        P(),
        P(("grp", "kp")),
    )
    out_specs = (P(None, None, ("grp", "kp")), P(None, None, ("grp", "kp")))
    return jax.shard_map(local, mesh=mesh, in_specs=in_specs, out_specs=out_specs, check_vma=False)
```
